32 devices in a mesh: ctx: 16 (over z, y, core), wt: 2 (over x).
Axes of the slice: x: 2, y: 2, z: 4, core: 2. Of those that a mesh axis runs over, the one named last changes fastest.
Arguments:
- activations: bfloat16 [2, 16384, 1024], P('wt', 'ctx'), may hold values from -6 to 6
- block_order: int32 [32], replicated, may hold values from 0 to 31, as said below
- qkv_weight: bfloat16 [1024, 3072], P('wt'), may hold values from -0.1875 to 0.1875
- qv_bias: bfloat16 [2048], P('wt'), may hold values from -3 to 3
- proj_weight: bfloat16 [1024, 1024], P('wt'), may hold values from -0.1875 to 0.1875
- proj_bias: bfloat16 [1024], P('wt'), may hold values from -3 to 3
- up_weight: bfloat16 [4096, 1024], P('wt'), may hold values from -0.1875 to 0.1875
- up_bias: bfloat16 [4096], P('wt'), may hold values from -3 to 3
- down_weight: bfloat16 [4096, 1024], P('wt'), may hold values from -0.09375 to 0.09375
- down_bias: bfloat16 [1024], P('wt'), may hold values from -3 to 3
- norm_gains: bfloat16 [4, 1024], P(None, 'wt'), may hold values from 0.25 to 1.75
- norm_biases: bfloat16 [4, 1024], P(None, 'wt'), may hold values from -2 to 2
- cotangent: bfloat16 [2, 16384, 1024], P('wt', 'ctx'), may hold values from -6 to 6
Outputs:
- layer_output: bfloat16 [2, 16384, 1024], P('wt', 'ctx')
- input_grad: float32 [2, 16384, 1024], P('wt', 'ctx')
- grad_qkv: float32 [1024, 3072], P('wt')
- grad_qvbias: float32 [2048], P('wt')
- grad_proj: float32 [1024, 1024], P('wt')
- grad_projbias: float32 [1024], P('wt')
- grad_upward: float32 [4096, 1024], P('wt')
- grad_upbias: float32 [4096], P('wt')
- grad_downward: float32 [4096, 1024], P('wt')
- grad_downbias: float32 [1024], P('wt')
- grad_gains: float32 [4, 1024], P(None, 'wt')
- grad_biases: float32 [4, 1024], P(None, 'wt')
The draws below stay inside these ranges and needn't reach their ends.
Inputs may be any that keep to these rules, and one draw needn't show every extreme that they name: `block_order`: for each index d of ctx, slots 2 d and 2 d + 1 hold blocks m and 31 - m for some m below 16, so that every block is held once; all sequences use the same order.
All inputs are finite; a program needn't handle non-finite values.
Results may differ from the reference program's by a relative error of at most 0.02.
Values may be sent and summed in bfloat16 or wider, within the bound.
No kernel may reach another device: no remote copies, remote signals or barrier semaphores. Data moves between devices by JAX's collectives and lax.ppermute only.
A program may use at most 704 MiB of HBM per device.

```python
import math
import jax
import jax.numpy as jnp
from jax import lax

D = 1024
HEADS = 16
HEAD_DIM = 64
FF = 4096
SEQ_LEN = 16384
BLOCKS = 32
BLK = 512
SEQS = 2


def draw_block_order(key, part):
    pair_count = BLOCKS // 2
    low_blocks = jax.random.permutation(key, pair_count).astype(jnp.int32)
    high_blocks = (BLOCKS - 1 - low_blocks).astype(jnp.int32)
    return jnp.stack([low_blocks, high_blocks], axis=1).reshape(BLOCKS)


def level_of(stream_key, shape, cuts, least, largest):
    def one(axis_at, shards_of):
        draws = jax.random.uniform(jax.random.fold_in(jax.random.fold_in(stream_key, 6), axis_at), (shards_of,), jnp.float32, least / len(cuts), largest / len(cuts))
        return jnp.repeat(jnp.exp(draws), shape[axis_at] // shards_of).reshape((-1,) + (1,) * (len(shape) - axis_at - 1))

    loudness = one(*cuts[0])
    for cut in cuts[1:]:
        loudness = loudness * one(*cut)
    return loudness


def gaussian(own_key, extent, deviation, limit, pieces=(), held_as=jnp.bfloat16):
    factor_of = level_of(own_key, extent, pieces, -0.22, 0.18) if pieces else 1.0
    array = jax.random.normal(own_key, extent, jnp.float32) * deviation * factor_of
    return jnp.minimum(jnp.maximum(array, -limit), limit).astype(held_as)


def setup_inputs(seed: int = 0) -> dict:
    streams_of = jax.random.split(jax.random.key(seed), 14)
    activations = gaussian(streams_of[0], (SEQS, SEQ_LEN, D), 1.0, 6.0, ((0, 2), (1, 16)))
    block_order = draw_block_order(jax.random.fold_in(streams_of[13], 71), 0)
    qkv_weight = gaussian(streams_of[2], (D, 3 * D), D ** -0.5, 0.1875, ((0, 2),))
    qv_bias = gaussian(streams_of[3], (2 * D,), 0.5, 3.0, ((0, 2),))
    proj_weight = gaussian(streams_of[4], (D, D), D ** -0.5, 0.1875, ((0, 2),))
    proj_bias = gaussian(streams_of[5], (D,), 0.5, 3.0, ((0, 2),))
    up_weight = gaussian(streams_of[6], (FF, D), D ** -0.5, 0.1875, ((0, 2),))
    up_bias = gaussian(streams_of[7], (FF,), 0.5, 3.0, ((0, 2),))
    down_weight = gaussian(streams_of[8], (FF, D), FF ** -0.5, 0.09375, ((0, 2),))
    down_bias = gaussian(streams_of[9], (D,), 0.5, 3.0, ((0, 2),))
    norm_gains = jnp.clip(1.0 + 0.15 * jax.random.normal(streams_of[10], (4, D), jnp.float32), 0.25, 1.75).astype(jnp.bfloat16)
    norm_biases = gaussian(streams_of[11], (4, D), 0.3, 2.0, ((1, 2),))
    cotangent = gaussian(streams_of[12], (SEQS, SEQ_LEN, D), 1.0, 6.0, ((0, 2), (1, 16)))
    return {"activations": activations, "block_order": block_order, "qkv_weight": qkv_weight, "qv_bias": qv_bias, "proj_weight": proj_weight, "proj_bias": proj_bias, "up_weight": up_weight, "up_bias": up_bias, "down_weight": down_weight, "down_bias": down_bias, "norm_gains": norm_gains, "norm_biases": norm_biases, "cotangent": cotangent}


@jax.custom_vjp
def low(v):
    return lax.optimization_barrier(v.astype(jnp.bfloat16)).astype(jnp.float32)

@jax.custom_vjp
def low_back(v):
    return v

def low_keep(v):
    return (low(v), None)

def low_pass(kept, grad):
    return (grad,)

def back_keep(v):
    return (v, None)

def back_low(kept, grad):
    return (low(grad),)
low.defvjp(low_keep, low_pass)
low_back.defvjp(back_keep, back_low)
relax_alpha = 32.0
norm_eps = 1e-05
huge_negative = -1e+30
highest = lax.Precision.HIGHEST

def layer_norm(values, norm_gain, norm_shift):
    average = lax.optimization_barrier(jnp.mean(values, axis=-1, keepdims=True))
    centered = values - average
    variance = lax.optimization_barrier(jnp.mean(centered * centered, axis=-1, keepdims=True))
    return centered * lax.rsqrt(variance + norm_eps) * norm_gain + norm_shift

def attend_block(query_block, query_pos, key_rows, value_rows, key_pos):
    raw_scores = jnp.einsum('qhd,khd->hqk', query_block, key_rows, precision=highest)
    raw_scores = low_back(raw_scores)
    visible = query_pos[:, None] >= key_pos[None, :]
    masked = jnp.where(visible[None, :, :], raw_scores, huge_negative)
    shifted = relax_alpha * (masked - lax.optimization_barrier(jnp.max(masked, axis=-1, keepdims=True)))
    expo = jnp.exp(shifted)
    probs_full = expo / lax.optimization_barrier(jnp.sum(expo, axis=-1, keepdims=True))
    return jnp.einsum('hqk,khd->qhd', low(probs_full), value_rows, precision=highest)

def sequence_forward(param_set, x_seq, positions):
    qkv_weight, qv_bias, proj_weight, proj_bias, up_weight, up_bias, down_weight, down_bias, norm_gains, norm_biases = param_set
    length = x_seq.shape[0]
    model_width = x_seq.shape[1]
    normed = low(layer_norm(x_seq, norm_gains[0], norm_biases[0]))
    projected = jnp.dot(normed, qkv_weight, precision=highest)
    query_scale = 1.0 / (relax_alpha * math.sqrt(HEAD_DIM))
    scaled = low(low_back((projected[:, :model_width] + qv_bias[:model_width]) * query_scale))
    key_rows = low(low_back(projected[:, model_width:2 * model_width])).reshape(length, HEADS, HEAD_DIM)
    value_rows = low(low_back(projected[:, 2 * model_width:] + qv_bias[model_width:])).reshape(length, HEADS, HEAD_DIM)
    qblock_rows = math.gcd(length, 512)
    block_count = length // qblock_rows
    query_blocks = scaled.reshape(block_count, qblock_rows, HEADS, HEAD_DIM)
    pos_blocks = positions.reshape(block_count, qblock_rows)

    def one_block(operands):
        return attend_block(operands[0], operands[1], key_rows, value_rows, positions)
    attended = lax.map(jax.checkpoint(one_block), (query_blocks, pos_blocks)).reshape(length, model_width)
    attended = low(low_back(attended))
    projected_out = low_back(jnp.dot(attended, proj_weight, precision=highest) + proj_bias)
    residual = x_seq + layer_norm(projected_out, norm_gains[1], norm_biases[1])
    normed_mid = low(layer_norm(residual, norm_gains[2], norm_biases[2]))
    pre_act = low_back(jnp.dot(normed_mid, up_weight.T, precision=highest) + up_bias)
    hidden = low(jax.nn.gelu(pre_act, approximate=True))
    branch = low_back(jnp.dot(hidden, down_weight, precision=highest) + down_bias)
    return residual + layer_norm(branch, norm_gains[3], norm_biases[3])

def reference(activations, block_order, qkv_weight, qv_bias, proj_weight, proj_bias, up_weight, up_bias, down_weight, down_bias, norm_gains, norm_biases, cotangent):
    offsets = jnp.arange(BLK, dtype=jnp.int32)
    positions = (block_order.astype(jnp.int32)[:, None] * BLK + offsets[None, :]).reshape(-1).astype(jnp.int32)
    params = tuple((weight.astype(jnp.float32) for weight in (qkv_weight, qv_bias, proj_weight, proj_bias, up_weight, up_bias, down_weight, down_bias, norm_gains, norm_biases)))
    inputs = activations.astype(jnp.float32)

    def whole_layer(param_set, layer_in):

        def seq_step(carried, x_seq):
            return (carried, sequence_forward(param_set, x_seq, positions))
        carried, results = lax.scan(seq_step, jnp.zeros((), jnp.float32), layer_in)
        return results
    outputs, pullback = jax.vjp(whole_layer, params, inputs)
    param_grads, input_grad = pullback(cotangent.astype(jnp.float32))
    return (outputs.astype(jnp.bfloat16), input_grad, param_grads[0], param_grads[1], param_grads[2], param_grads[3], param_grads[4], param_grads[5], param_grads[6], param_grads[7], param_grads[8], param_grads[9])
```

```python
import functools
import math

import jax
import jax.numpy as jnp
from jax import lax
from jax.experimental import pallas as pl
from jax.experimental.pallas import tpu as pltpu
from jax.sharding import Mesh
from jax.sharding import PartitionSpec as P

HEADS = 16
ALPHA = 32.0
EPS = 1e-05
NEG = -1e30
bf16 = jnp.bfloat16
f32 = jnp.float32
MIB = 1 << 20


def layer_norm(values, norm_gain, norm_shift):
    average = jnp.mean(values, axis=-1, keepdims=True)
    centered = values - average
    variance = jnp.mean(centered * centered, axis=-1, keepdims=True)
    return centered * lax.rsqrt(variance + EPS) * norm_gain + norm_shift


def norm_backward(values, norm_gain, norm_shift, upstream):
    _, pullback = jax.vjp(layer_norm, values, norm_gain, norm_shift)
    return pullback(upstream)


def gelu_tanh(values):
    return jax.nn.gelu(values, approximate=True)


def gelu_backward(values, upstream):
    _, pullback = jax.vjp(gelu_tanh, values)
    return pullback(upstream)[0]


def dot(a, b, ca, cb):
    return lax.dot_general(a, b, (((ca,), (cb,)), ((), ())), preferred_element_type=f32)


def columns(index, width):
    return pl.ds(pl.multiple_of(index * width, width), width)


def whole(shape):
    return pl.BlockSpec(shape, lambda *_: (0,) * len(shape), pipeline_mode=pl.Buffered(1))


def project_kernel(table, a1_first, a1_second, weight, bias, q_t, k_n, v_t):
    width = k_n.shape[1]
    blk = a1_first.shape[0]
    for half, rows in enumerate((a1_first, a1_second)):
        part = slice(half * blk, (half + 1) * blk)
        heads = dot(rows[...], weight[...], 1, 0) + bias[...]
        turned = jnp.transpose(heads)
        q_t[:, part] = (turned[:width] * 0.125).astype(bf16)
        v_t[:, part] = turned[2 * width :].astype(bf16)
        k_n[part, :] = heads[:, width : 2 * width].astype(bf16)


def project(table, a1_full, weight, bias, blk, width):
    tokens, model = a1_full.shape
    tile = 2 * blk
    turned = pl.BlockSpec((width, tile), lambda i, t: (0, i))
    straight = pl.BlockSpec((tile, width), lambda i, t: (i, 0))
    return pl.pallas_call(
        project_kernel,
        grid_spec=pltpu.PrefetchScalarGridSpec(
            num_scalar_prefetch=1,
            grid=(tokens // tile,),
            in_specs=[
                pl.BlockSpec((blk, model), lambda i, t: (t[2 * i], 0)),
                pl.BlockSpec((blk, model), lambda i, t: (t[2 * i + 1], 0)),
                whole(weight.shape),
                whole(bias.shape),
            ],
            out_specs=[turned, straight, turned],
        ),
        out_shape=[
            jax.ShapeDtypeStruct((width, tokens), bf16),
            jax.ShapeDtypeStruct((tokens, width), bf16),
            jax.ShapeDtypeStruct((width, tokens), bf16),
        ],
        compiler_params=pltpu.CompilerParams(vmem_limit_bytes=48 * MIB),
        cost_estimate=pl.CostEstimate(
            flops=8 * tokens * model * width, bytes_accessed=2 * tokens * model, transcendentals=0
        ),
        name="project",
    )(table, a1_full, a1_full, weight, bias)


def forward_kernel(base, table, q_t, k_n, v_t, out_t, log_total, out_slots, scores):
    _, width, blk = out_slots.shape
    tile = q_t.shape[1]
    step = base + pl.program_id(0)
    query = q_t[...]

    def score(index):
        return dot(k_n[columns(index, blk), :], query, 1, 0)

    def prepare(index, slot):
        tile_scores = score(index)
        scores[slot] = tile_scores
        return jnp.max(tile_scores, axis=0, keepdims=True)

    def absorb(index, slot, peak, total, summed, tile_peak):
        new_peak = jnp.maximum(peak, tile_peak)
        weights = jnp.exp(scores[slot] - new_peak)
        keep = jnp.exp(peak - new_peak)
        total = total * keep + jnp.sum(weights, axis=0, keepdims=True)
        summed = summed * keep + dot(v_t[:, columns(index, blk)], weights.astype(bf16), 1, 0)
        return new_peak, total, summed

    def body(pair, carry):
        peak, total, summed, tile_peak = carry
        for slot in range(2):
            next_peak = prepare(2 * pair + slot + 1, 1 - slot)
            peak, total, summed = absorb(2 * pair + slot, slot, peak, total, summed, tile_peak)
            tile_peak = next_peak
        return peak, total, summed, tile_peak

    carry = (
        jnp.full((1, tile), -jnp.inf, f32),
        jnp.zeros((1, tile), f32),
        jnp.zeros((width, tile), f32),
        prepare(0, 0),
    )
    peak, total, summed, _ = lax.fori_loop(0, step, body, carry)
    for half in range(2):
        index = 2 * step + half
        key_pos = half * blk + lax.broadcasted_iota(jnp.int32, (blk, tile), 0)
        query_pos = lax.broadcasted_iota(jnp.int32, (blk, tile), 1)
        tile_scores = jnp.where(query_pos >= key_pos, score(index), NEG)
        scores[half] = tile_scores
        tile_peak = jnp.max(tile_scores, axis=0, keepdims=True)
        peak, total, summed = absorb(index, half, peak, total, summed, tile_peak)
    result = summed / total
    out_t[...] = result
    log_total[...] = peak + jnp.log(total)
    low = result.astype(bf16)
    for half in range(2):
        out_slots[table[2 * step + half]] = low[:, half * blk : (half + 1) * blk]


def forward(high, table, q_t, k_n, v_t, blk):
    width, tokens = q_t.shape
    slots = tokens // (2 * blk)
    tile = 2 * blk
    steps = slots // 2
    base = steps if high else 0
    seen = tokens if high else tokens // 2
    return pl.pallas_call(
        functools.partial(forward_kernel, base),
        grid_spec=pltpu.PrefetchScalarGridSpec(
            num_scalar_prefetch=1,
            grid=(steps,),
            in_specs=[
                pl.BlockSpec((width, tile), lambda i, t: (0, base + i)),
                whole((seen, width)),
                whole((width, seen)),
            ],
            out_specs=[
                pl.BlockSpec((width, tile), lambda i, t: (0, i)),
                pl.BlockSpec((1, tile), lambda i, t: (0, i)),
                whole((slots, width, blk)),
            ],
            scratch_shapes=[pltpu.VMEM((2, blk, tile), f32)],
        ),
        out_shape=[
            jax.ShapeDtypeStruct((width, tokens // 2), f32),
            jax.ShapeDtypeStruct((1, tokens // 2), f32),
            jax.ShapeDtypeStruct((slots, width, blk), bf16),
        ],
        compiler_params=pltpu.CompilerParams(vmem_limit_bytes=56 * MIB),
        cost_estimate=pl.CostEstimate(
            flops=(6 if high else 2) * tokens * tokens * width,
            bytes_accessed=12 * tokens * width,
            transcendentals=(3 if high else 1) * tokens * tokens // 8,
        ),
        name="forward_high" if high else "forward_low",
    )(table, q_t, k_n, v_t)


def delta_kernel(table, given, out_t, q_t, grad_t, grad_n, delta, q_n):
    block = given[0]
    grad_t[...] = block
    wide = block.astype(f32)
    delta[...] = jnp.sum(wide * out_t[...], axis=0, keepdims=True)
    grad_n[...] = jnp.transpose(wide).astype(bf16)
    q_n[...] = jnp.transpose(q_t[...].astype(f32)).astype(bf16)


def delta_rows(high, table, given, out_t, q_t):
    slots, width, blk = given.shape
    half = slots * blk
    base = slots if high else 0
    return pl.pallas_call(
        delta_kernel,
        grid_spec=pltpu.PrefetchScalarGridSpec(
            num_scalar_prefetch=1,
            grid=(slots,),
            in_specs=[
                pl.BlockSpec((1, width, blk), lambda p, t: (t[base + p], 0, 0)),
                pl.BlockSpec((width, blk), lambda p, t: (0, p)),
                pl.BlockSpec((width, blk), lambda p, t: (0, base + p)),
            ],
            out_specs=[
                pl.BlockSpec((width, blk), lambda p, t: (0, p)),
                pl.BlockSpec((blk, width), lambda p, t: (p, 0)),
                pl.BlockSpec((1, blk), lambda p, t: (0, p)),
                pl.BlockSpec((blk, width), lambda p, t: (p, 0)),
            ],
        ),
        out_shape=[
            jax.ShapeDtypeStruct((width, half), bf16),
            jax.ShapeDtypeStruct((half, width), bf16),
            jax.ShapeDtypeStruct((1, half), f32),
            jax.ShapeDtypeStruct((half, width), bf16),
        ],
        compiler_params=pltpu.CompilerParams(vmem_limit_bytes=32 * MIB),
        name="delta_high" if high else "delta_low",
    )(table, given, out_t, q_t)


def backward_kernel(kind, base, after, *refs):
    table, q_t, q_n, grad_t, grad_n, log_total, delta, k_n, v_t = refs[:9]
    refs = refs[9:]
    cross = kind in ("first", "second")
    query_out = key_out = value_out = None
    if cross:
        (query_start, key_start, value_start), refs = refs[:3], refs[3:]
    if kind == "second":
        earlier, refs = refs[0], refs[1:]
    refs = refs[after:]
    if kind in ("high", "first"):
        query_out, refs = refs[0], refs[1:]
    elif kind == "low":
        (key_out, value_out), refs = refs[:2], refs[2:]
    out_slots, refs = refs[0], refs[1:]
    scores, grads, query_sum, key_sum, value_sum = refs
    slots, _, blk = out_slots.shape
    tile, width = k_n.shape
    step = pl.program_id(0)

    @pl.when(step == 0)
    def _():
        if cross:
            query_sum[...] = query_start[...]
        else:
            query_sum[...] = jnp.zeros_like(query_sum)
        if kind == "second":
            out_slots[:, width:] = earlier[...]

    keys = k_n[...]
    keys_t = jnp.transpose(keys.astype(f32)).astype(bf16)
    values = jnp.transpose(v_t[...].astype(f32)).astype(bf16)
    if cross:
        key_sum[...] = key_start[...]
        value_sum[...] = value_start[...]
    else:
        key_sum[...] = jnp.zeros_like(key_sum)
        value_sum[...] = jnp.zeros_like(value_sum)

    def prepare(index, slot):
        at = columns(index, blk)
        scores[slot] = dot(keys, q_t[:, at], 1, 0)
        grads[slot] = dot(values, grad_t[:, at], 1, 0)

    def absorb(index, slot, diagonal):
        at = columns(index, blk)
        tile_scores = scores[slot]
        if diagonal is not None:
            key_pos = lax.broadcasted_iota(jnp.int32, (tile, blk), 0)
            query_pos = diagonal * blk + lax.broadcasted_iota(jnp.int32, (tile, blk), 1)
            tile_scores = jnp.where(query_pos >= key_pos, tile_scores, NEG)
        probs = jnp.exp(tile_scores - log_total[:, at])
        score_grads = (probs * (grads[slot] - delta[:, at])).astype(bf16)
        value_sum[...] += dot(probs.astype(bf16), grad_n[at, :], 1, 0)
        key_sum[...] += dot(score_grads, q_n[at, :], 1, 0)
        query_sum[:, at] += dot(keys_t, score_grads, 1, 0)

    def sweep(first, pairs):
        prepare(first, 0)

        def body(pair, carry):
            index = first + 2 * pair
            prepare(index + 1, 1)
            absorb(index, 0, None)
            prepare(jnp.minimum(index + 2, slots - 1), 0)
            absorb(index + 1, 1, None)
            return carry

        lax.fori_loop(0, pairs, body, 0)

    if cross:
        sweep(0, slots // 2)
    else:
        for half in range(2):
            prepare(2 * step + half, half)
            absorb(2 * step + half, half, half)

        @pl.when(2 * step + 2 < slots)
        def _():
            sweep(2 * step + 2, slots // 2 - 1 - step)

    def halves():
        for half in range(2):
            yield table[base + 2 * step + half], slice(half * blk, (half + 1) * blk), half

    if kind == "low":
        key_out[...] = key_sum[...]
        value_out[...] = value_sum[...]
        for slot, _, half in halves():
            own = query_sum[:, columns(2 * step + half, blk)] * 0.125
            out_slots[slot] = own.astype(bf16)
    else:
        start = width if kind == "second" else 0
        key_t = jnp.transpose(key_sum[...]).astype(bf16)
        value_t = jnp.transpose(value_sum[...]).astype(bf16)
        for slot, part, _ in halves():
            out_slots[slot, start : start + width] = key_t[:, part]
            out_slots[slot, start + width : start + 2 * width] = value_t[:, part]
    if query_out is not None:

        @pl.when(step == pl.num_programs(0) - 1)
        def _():
            query_out[...] = query_sum[...]

    if kind == "second":

        @pl.when(step == pl.num_programs(0) - 1)
        def _():
            def finish(index, carry):
                own = query_sum[:, columns(index, blk)] * 0.125
                out_slots[table[slots + index], 0:width] = own.astype(bf16)
                return carry

            lax.fori_loop(0, slots, finish, 0)


def backward(kind, table, queries, k_n, v_t, starts, after, blk):
    width, half = queries[0].shape
    slots = half // blk
    tile = 2 * blk
    cross = kind in ("first", "second")
    steps = slots // 4 if cross else slots // 2
    skip = {"high": slots // 2, "low": 0, "first": 0, "second": slots // 4}[kind]
    start_skip = skip if cross else 0
    straight = pl.BlockSpec((tile, width), lambda i, t: (start_skip + i, 0))
    in_specs = [whole(array.shape) for array in queries] + [
        pl.BlockSpec((tile, width), lambda i, t: (skip + i, 0)),
        pl.BlockSpec((width, tile), lambda i, t: (0, skip + i)),
    ]
    if cross:
        in_specs += [whole((width, half)), straight, straight]
    if kind == "second":
        in_specs += [whole(starts[3].shape)]
    in_specs += [pl.BlockSpec(memory_space=pl.ANY)] * len(after)
    rows = {"high": 2, "low": 1, "first": 2, "second": 3}[kind] * width
    out_specs = [whole((slots, rows, blk))]
    out_shape = [jax.ShapeDtypeStruct((slots, rows, blk), bf16)]
    if kind in ("high", "first"):
        out_specs = [whole((width, half))] + out_specs
        out_shape = [jax.ShapeDtypeStruct((width, half), f32)] + out_shape
    elif kind == "low":
        out_specs = [straight, straight] + out_specs
        out_shape = [jax.ShapeDtypeStruct((half, width), f32)] * 2 + out_shape
    return pl.pallas_call(
        functools.partial(backward_kernel, kind, 2 * skip, len(after)),
        grid_spec=pltpu.PrefetchScalarGridSpec(
            num_scalar_prefetch=1,
            grid=(steps,),
            in_specs=in_specs,
            out_specs=out_specs,
            scratch_shapes=[
                pltpu.VMEM((2, tile, blk), f32),
                pltpu.VMEM((2, tile, blk), f32),
                pltpu.VMEM((width, half), f32),
                pltpu.VMEM((tile, width), f32),
                pltpu.VMEM((tile, width), f32),
            ],
        ),
        out_shape=out_shape,
        compiler_params=pltpu.CompilerParams(vmem_limit_bytes=56 * MIB),
        cost_estimate=pl.CostEstimate(
            flops=4 * half * half * width,
            bytes_accessed=32 * half * width,
            transcendentals=half * half // 8,
        ),
        name="backward_" + kind,
    )(table, *queries, k_n, v_t, *starts, *after)


def weight_kernel(high_pair, low_query, rest, a1, total):
    blk = rest.shape[2]
    width = low_query.shape[1]

    @pl.when(pl.program_id(0) == 0)
    def _():
        total[...] = jnp.zeros_like(total)

    low = jnp.concatenate([low_query[0], rest[0, width:]], axis=0)
    high = jnp.concatenate([rest[0, :width], high_pair[0]], axis=0)
    total[...] += dot(low, a1[:blk], 1, 0) + dot(high, a1[blk:], 1, 0)


def weight_grad(high_pair, low_query, rest, a1_full):
    slots, rows, blk = rest.shape
    tokens, model = a1_full.shape
    return pl.pallas_call(
        weight_kernel,
        grid=(slots,),
        in_specs=[
            pl.BlockSpec((1,) + high_pair.shape[1:], lambda s: (s, 0, 0)),
            pl.BlockSpec((1,) + low_query.shape[1:], lambda s: (s, 0, 0)),
            pl.BlockSpec((1, rows, blk), lambda s: (s, 0, 0)),
            pl.BlockSpec((2 * blk, model), lambda s: (s, 0)),
        ],
        out_specs=pl.BlockSpec((rows, model), lambda s: (0, 0)),
        out_shape=jax.ShapeDtypeStruct((rows, model), f32),
        compiler_params=pltpu.CompilerParams(vmem_limit_bytes=48 * MIB),
        cost_estimate=pl.CostEstimate(
            flops=2 * rows * tokens * model, bytes_accessed=2 * tokens * model, transcendentals=0
        ),
        name="weight_grad",
    )(high_pair, low_query, rest, a1_full)


def local(
    groups,
    activations,
    block_order,
    qkv_weight,
    qv_bias,
    proj_weight,
    proj_bias,
    up_weight,
    up_bias,
    down_weight,
    down_bias,
    norm_gains,
    norm_biases,
    cotangent,
):
    _, rows, model = activations.shape
    blk = rows // 2
    width = model // HEADS
    ctx = ("r", "h")
    everywhere = ("r", "h", "wt")
    devices = groups * HEADS
    weight_parts = lax.axis_size("wt")
    head = lax.axis_index("h")
    group = lax.axis_index("r")
    part = lax.axis_index("wt")

    small = (qv_bias, proj_bias, up_bias, down_bias, norm_gains, norm_biases)
    packed = jnp.concatenate([array.reshape(-1) for array in small])
    gathered = lax.all_gather(packed, "wt", axis=0)
    pieces, start = [], 0
    for array in small:
        piece = gathered[:, start : start + array.size].reshape((weight_parts,) + array.shape)
        start += array.size
        if array.ndim == 2:
            piece = jnp.transpose(piece, (1, 0, 2)).reshape(array.shape[0], -1)
        else:
            piece = piece.reshape(-1)
        pieces.append(piece.astype(f32))
    qvbias, projbias, upbias, downbias, gains, shifts = pieces

    inputs = activations.reshape(rows, model).astype(f32)
    upstream = cotangent.reshape(rows, model).astype(f32)
    a1 = layer_norm(inputs, gains[0], shifts[0]).astype(bf16)
    a1_full = lax.all_gather(a1, ctx, axis=0, tiled=True)

    mine = lax.dynamic_index_in_dim(
        qkv_weight.reshape(-1, 3, HEADS, width), head, axis=2, keepdims=False
    )
    mine = lax.all_gather(mine.reshape(-1, 3 * width), "wt", axis=0, tiled=True)
    q_bias = lax.dynamic_slice(qvbias, (head * width,), (width,))
    v_bias = lax.dynamic_slice(qvbias, (model + head * width,), (width,))
    bias = jnp.concatenate([q_bias, jnp.zeros_like(q_bias), v_bias])

    lows = block_order.reshape(devices, 2)[:, 0]
    numbers = jnp.arange(devices, dtype=jnp.int32)
    owner = jnp.sum(jnp.where(lows[None, :] == numbers[:, None], numbers[None, :], 0), axis=1)
    owner = jnp.concatenate([owner, owner[::-1]]).astype(jnp.int32)
    is_high = (jnp.arange(2 * devices, dtype=jnp.int32) >= devices).astype(jnp.int32)
    slot_of = 2 * owner + is_high

    half = devices * blk
    q_t, k_n, v_t = project(slot_of, a1_full, mine, bias[None, :], blk, width)
    out_low, log_low, slots_low = forward(False, owner, q_t, k_n, v_t, blk)
    out_high, log_high, slots_high = forward(True, owner, q_t, k_n, v_t, blk)

    def to_tokens(array):
        own = lax.dynamic_slice_in_dim(array, group * HEADS, HEADS, 0)
        return lax.all_to_all(own, "h", 0, 0, tiled=True).reshape(-1, blk)

    def to_heads(array):
        array = lax.all_to_all(array.reshape(HEADS, width, blk), "h", 0, 0, tiled=True)
        if groups > 1:
            array = lax.all_gather(array, "r", axis=0, tiled=True)
        return array

    attended_t = jnp.concatenate([to_tokens(slots_low), to_tokens(slots_high)], axis=1)

    full_proj = lax.all_gather(proj_weight, "wt", axis=0, tiled=True)
    up_full = lax.all_gather(up_weight, "wt", axis=0, tiled=True)
    down_full = lax.all_gather(down_weight, "wt", axis=0, tiled=True)
    full_qkv = lax.all_gather(qkv_weight, "wt", axis=0, tiled=True)

    proj_pre = dot(attended_t, full_proj, 0, 0) + projbias
    residual = inputs + layer_norm(proj_pre, gains[1], shifts[1])
    normed_mid = layer_norm(residual, gains[2], shifts[2]).astype(bf16)
    pre_act = dot(normed_mid, up_full, 1, 1) + upbias
    hidden = gelu_tanh(pre_act).astype(bf16)
    branch = dot(hidden, down_full, 1, 0) + downbias
    layer_output = (residual + layer_norm(branch, gains[3], shifts[3])).astype(bf16)

    grad_branch, gain_three, shift_three = norm_backward(branch, gains[3], shifts[3], upstream)
    grad_branch = grad_branch.astype(bf16)
    grad_hidden = dot(grad_branch, down_full, 1, 1)
    grad_pre = gelu_backward(pre_act, grad_hidden).astype(bf16)
    grad_mid = dot(grad_pre, up_full, 1, 0)
    grad_residual, gain_two, shift_two = norm_backward(residual, gains[2], shifts[2], grad_mid)
    grad_residual = upstream + grad_residual
    grad_proj_pre, gain_one, shift_one = norm_backward(
        proj_pre, gains[1], shifts[1], grad_residual
    )
    grad_proj_pre = grad_proj_pre.astype(bf16)
    grad_attended_t = dot(full_proj, grad_proj_pre, 1, 1).astype(bf16)
    given_high = to_heads(grad_attended_t[:, blk:])
    given_low = to_heads(grad_attended_t[:, :blk])

    grad_downward = dot(hidden, grad_branch, 0, 0).astype(bf16)
    grad_upward = dot(grad_pre, normed_mid, 0, 0).astype(bf16)
    grad_proj = dot(attended_t, grad_proj_pre, 1, 0).astype(bf16)

    def own_rows(array):
        length = array.shape[0] // weight_parts
        return lax.dynamic_slice_in_dim(array, part * length, length, 0)

    early = jnp.concatenate(
        [
            jnp.sum(grad_pre.astype(f32), axis=0),
            jnp.sum(grad_branch.astype(f32), axis=0),
            jnp.sum(grad_proj_pre.astype(f32), axis=0),
            gain_one,
            gain_two,
            gain_three,
            shift_one,
            shift_two,
            shift_three,
        ]
    ).astype(bf16)
    grad_proj = jnp.concatenate([grad_proj, early.reshape(-1, model)], axis=0)
    given_high, given_low, grad_downward, grad_upward, grad_proj = lax.optimization_barrier(
        (given_high, given_low, grad_downward, grad_upward, grad_proj)
    )
    summed = lax.psum((grad_downward, grad_upward, grad_proj), everywhere)
    grad_downward, grad_upward, grad_proj = summed
    early = grad_proj[model:].astype(f32).reshape(-1)
    grad_proj = grad_proj[:model]
    grad_downward = own_rows(grad_downward).astype(f32)
    grad_upward = own_rows(grad_upward).astype(f32)
    grad_proj = own_rows(grad_proj).astype(f32)
    hidden_width = up_full.shape[0]
    grad_upbias = own_rows(early[:hidden_width])
    early = early[hidden_width:].reshape(8, model)
    grad_downbias = own_rows(early[0])
    grad_projbias = own_rows(early[1])

    def token_grads(array):
        own = lax.dynamic_slice_in_dim(array, group * HEADS, HEADS, 0)
        own = lax.all_to_all(own, "h", 0, 0, tiled=True).reshape(HEADS, -1, width, blk)
        return jnp.transpose(own, (1, 0, 2, 3)).reshape(-1, blk)

    grad_t, grad_n, delta, q_n = delta_rows(True, owner, given_high, out_high, q_t)
    high = (q_t[:, half:], q_n, grad_t, grad_n, log_high, delta)
    query_sum, high_pair = backward("high", owner, high, k_n, v_t, (), (), blk)
    high_tokens = token_grads(high_pair)
    grad_t, grad_n, delta, q_n = delta_rows(False, owner, given_low, out_low, q_t)
    low = (q_t[:, :half], q_n, grad_t, grad_n, log_low, delta)
    key_sum, value_sum, low_query = backward("low", owner, low, k_n, v_t, (), (), blk)
    low_tokens = token_grads(low_query)
    starts = (query_sum, key_sum, value_sum)
    query_sum, earlier = backward(
        "first", owner, high, k_n, v_t, starts, (high_tokens,), blk
    )
    starts = (query_sum, key_sum, value_sum, earlier)
    after = (low_tokens,) + tuple(summed)
    (rest,) = backward("second", owner, high, k_n, v_t, starts, after, blk)
    rest_tokens = token_grads(rest)

    columns_grad = weight_grad(high_pair, low_query, rest, a1_full).T.astype(bf16)
    columns_grad = columns_grad.reshape(weight_parts, -1, 3 * width)
    columns_grad = lax.all_to_all(columns_grad, "wt", 0, 0, tiled=True)
    columns_grad = jnp.sum(columns_grad.astype(f32), axis=0).astype(bf16)
    all_columns = lax.all_gather(columns_grad, "h", axis=0)
    all_columns = all_columns.reshape(HEADS, -1, 3, width)
    grad_qkv = jnp.transpose(all_columns, (1, 2, 0, 3)).reshape(-1, 3 * model).astype(f32)

    grads_t = jnp.concatenate(
        [
            jnp.concatenate([low_tokens, rest_tokens[model:]], axis=0),
            jnp.concatenate([rest_tokens[:model], high_tokens], axis=0),
        ],
        axis=1,
    )
    grad_normed = dot(grads_t, full_qkv, 0, 1)
    grad_inputs, gain_zero, shift_zero = norm_backward(inputs, gains[0], shifts[0], grad_normed)
    input_grad = (grad_residual + grad_inputs).reshape(1, rows, model)
    bias_sums = jnp.sum(grads_t.astype(f32), axis=1)

    def own_columns(array):
        length = array.shape[1] // weight_parts
        return lax.dynamic_slice_in_dim(array, part * length, length, 1)

    late = jnp.concatenate([bias_sums[:model], bias_sums[2 * model :], gain_zero, shift_zero])
    late = jnp.concatenate(
        [
            late[: 2 * model].reshape(weight_parts, -1),
            late[2 * model : 3 * model].reshape(weight_parts, -1),
            late[3 * model :].reshape(weight_parts, -1),
        ],
        axis=1,
    )
    late = jnp.broadcast_to(late[None], (devices,) + late.shape)
    late = late.reshape(devices * weight_parts, 1, -1)
    late = jnp.sum(lax.all_to_all(late, everywhere, 0, 0, tiled=True), axis=0)[0]
    length = model // weight_parts
    grad_qvbias = late[: 2 * length]
    late = late[2 * length :].reshape(2, length)
    early = own_columns(early)
    grad_gains = jnp.concatenate([late[0:1], early[2:5]], axis=0)
    grad_biases = jnp.concatenate([late[1:2], early[5:8]], axis=0)
    return (
        layer_output.reshape(1, rows, model),
        input_grad,
        grad_qkv,
        grad_qvbias,
        grad_proj,
        grad_projbias,
        grad_upward,
        grad_upbias,
        grad_downward,
        grad_downbias,
        grad_gains,
        grad_biases,
    )


def solution(mesh):
    groups = mesh.shape["ctx"] // HEADS
    split = Mesh(
        mesh.devices.reshape(groups, HEADS, mesh.shape["wt"]), ("r", "h", "wt")
    )
    tokens = P("wt", ("r", "h"), None)
    rows, flat, cols = P("wt", None), P("wt"), P(None, "wt")
    return jax.shard_map(
        functools.partial(local, groups),
        mesh=split,
        in_specs=(tokens, P(), rows, flat, rows, flat, rows, flat, rows, flat, cols, cols, tokens),
        out_specs=(tokens, tokens, rows, flat, rows, flat, rows, flat, rows, flat, cols, cols),
        check_vma=False,
    )
```

```python
import functools
import math

import jax
import jax.numpy as jnp
from jax import lax
from jax.experimental import pallas as pl
from jax.experimental.pallas import tpu as pltpu
from jax.sharding import Mesh
from jax.sharding import PartitionSpec as P

HEADS = 16
ALPHA = 32.0
EPS = 1e-05
NEG = -1e30
bf16 = jnp.bfloat16
f32 = jnp.float32
MIB = 1 << 20


def layer_norm(values, norm_gain, norm_shift):
    average = jnp.mean(values, axis=-1, keepdims=True)
    centered = values - average
    variance = jnp.mean(centered * centered, axis=-1, keepdims=True)
    return centered * lax.rsqrt(variance + EPS) * norm_gain + norm_shift


def norm_backward(values, norm_gain, norm_shift, upstream):
    _, pullback = jax.vjp(layer_norm, values, norm_gain, norm_shift)
    return pullback(upstream)


def gelu_and_slope(values):
    squared = values * values
    scale = math.sqrt(2.0 / math.pi)
    bent = jnp.tanh(scale * (values * (1.0 + 0.044715 * squared)))
    half = 0.5 * (1.0 + bent)
    slope = half + (0.5 * scale) * values * (1.0 - bent * bent) * (1.0 + 0.134145 * squared)
    return values * half, slope


def dot(a, b, ca, cb):
    return lax.dot_general(a, b, (((ca,), (cb,)), ((), ())), preferred_element_type=f32)


def columns(index, width):
    return pl.ds(pl.multiple_of(index * width, width), width)


def whole(shape):
    return pl.BlockSpec(shape, lambda *_: (0,) * len(shape), pipeline_mode=pl.Buffered(1))


def project_kernel(table, *refs):
    blocks, (weight, bias, q_t, k_n, v_t) = refs[:-5], refs[-5:]
    width = k_n.shape[1]
    for number, rows in enumerate(blocks):
        blk = rows.shape[0]
        part = slice(number * blk, (number + 1) * blk)
        heads = (dot(rows[...], weight[...], 1, 0) + bias[...]).astype(bf16)
        turned = jnp.transpose(heads[:, : 2 * width])
        q_t[:, part] = turned[:width]
        v_t[:, part] = turned[width:]
        k_n[part, :] = heads[:, 2 * width :]


def project(table, a1_full, weight, bias, blk, width):
    tokens, model = a1_full.shape
    count = 4
    tile = count * blk
    turned = pl.BlockSpec((width, tile), lambda i, t: (0, i))
    straight = pl.BlockSpec((tile, width), lambda i, t: (i, 0))

    def block(number):
        return pl.BlockSpec((blk, model), lambda i, t: (t[count * i + number], 0))

    return pl.pallas_call(
        project_kernel,
        grid_spec=pltpu.PrefetchScalarGridSpec(
            num_scalar_prefetch=1,
            grid=(tokens // tile,),
            in_specs=[block(number) for number in range(count)]
            + [whole(weight.shape), whole(bias.shape)],
            out_specs=[turned, straight, turned],
        ),
        out_shape=[
            jax.ShapeDtypeStruct((width, tokens), bf16),
            jax.ShapeDtypeStruct((tokens, width), bf16),
            jax.ShapeDtypeStruct((width, tokens), bf16),
        ],
        compiler_params=pltpu.CompilerParams(vmem_limit_bytes=48 * MIB),
        cost_estimate=pl.CostEstimate(
            flops=8 * tokens * model * width, bytes_accessed=2 * tokens * model, transcendentals=0
        ),
        name="project",
    )(table, *([a1_full] * count), weight, bias)


def forward_kernel(base, table, q_t, k_n, v_t, out_t, log_total, out_slots, scores):
    _, width, blk = out_slots.shape
    tile = q_t.shape[1]
    step = base + pl.program_id(0)
    query = q_t[...]

    def score(index):
        return dot(k_n[columns(index, blk), :], query, 1, 0)

    def prepare(index, slot):
        tile_scores = score(index)
        scores[slot] = tile_scores
        return jnp.max(tile_scores, axis=0, keepdims=True)

    def absorb(index, tile_scores, peak, total, summed, tile_peak):
        new_peak = jnp.maximum(peak, tile_peak)
        weights = jnp.exp(tile_scores - new_peak)
        keep = jnp.exp(peak - new_peak)
        total = total * keep + jnp.sum(weights, axis=0, keepdims=True)
        summed = summed * keep + dot(v_t[:, columns(index, blk)], weights.astype(bf16), 1, 0)
        return new_peak, total, summed

    def body(pair, carry):
        peak, total, summed, tile_peak = carry
        for slot in range(2):
            next_peak = prepare(2 * pair + slot + 1, 1 - slot)
            peak, total, summed = absorb(
                2 * pair + slot, scores[slot], peak, total, summed, tile_peak
            )
            tile_peak = next_peak
        return peak, total, summed, tile_peak

    carry = (
        jnp.full((1, tile), -jnp.inf, f32),
        jnp.zeros((1, tile), f32),
        jnp.zeros((width, tile), f32),
        prepare(0, 0),
    )
    peak, total, summed, _ = lax.fori_loop(0, step, body, carry)
    for half in range(2):
        part = query[:, half * blk :]
        shape = (blk, tile - half * blk)
        key_pos = lax.broadcasted_iota(jnp.int32, shape, 0)
        query_pos = lax.broadcasted_iota(jnp.int32, shape, 1)
        tile_scores = dot(k_n[columns(2 * step + half, blk), :], part, 1, 0)
        tile_scores = jnp.where(query_pos >= key_pos, tile_scores, NEG)
        tile_peak = jnp.max(tile_scores, axis=0, keepdims=True)
        state = absorb(2 * step + half, tile_scores, peak, total, summed, tile_peak)
        if half == 0:
            left = tuple(array[:, :blk] for array in state)
            peak, total, summed = (array[:, blk:] for array in state)
    peak, total, summed = (
        jnp.concatenate([first, second], axis=1) for first, second in zip(left, state)
    )
    result = summed / total
    out_t[...] = result
    log_total[...] = peak + jnp.log(total)
    low = result.astype(bf16)
    for half in range(2):
        out_slots[table[2 * step + half]] = low[:, half * blk : (half + 1) * blk]


def forward(high, table, q_t, k_n, v_t, blk):
    width, tokens = q_t.shape
    slots = tokens // (2 * blk)
    tile = 2 * blk
    steps = slots // 2
    base = steps if high else 0
    seen = tokens if high else tokens // 2
    return pl.pallas_call(
        functools.partial(forward_kernel, base),
        grid_spec=pltpu.PrefetchScalarGridSpec(
            num_scalar_prefetch=1,
            grid=(steps,),
            in_specs=[
                pl.BlockSpec((width, tile), lambda i, t: (0, base + i)),
                whole((seen, width)),
                whole((width, seen)),
            ],
            out_specs=[
                pl.BlockSpec((width, tile), lambda i, t: (0, i)),
                pl.BlockSpec((1, tile), lambda i, t: (0, i)),
                whole((slots, width, blk)),
            ],
            scratch_shapes=[pltpu.VMEM((2, blk, tile), f32)],
        ),
        out_shape=[
            jax.ShapeDtypeStruct((width, tokens // 2), f32),
            jax.ShapeDtypeStruct((1, tokens // 2), f32),
            jax.ShapeDtypeStruct((slots, width, blk), bf16),
        ],
        compiler_params=pltpu.CompilerParams(vmem_limit_bytes=56 * MIB),
        cost_estimate=pl.CostEstimate(
            flops=(6 if high else 2) * tokens * tokens * width,
            bytes_accessed=12 * tokens * width,
            transcendentals=(3 if high else 1) * tokens * tokens // 8,
        ),
        name="forward_high" if high else "forward_low",
    )(table, q_t, k_n, v_t)


def delta_kernel(table, given, out_t, q_t, grad_t, grad_n, delta, q_n):
    block = given[0]
    grad_t[...] = block
    wide = block.astype(f32)
    delta[...] = jnp.sum(wide * out_t[...], axis=0, keepdims=True)
    grad_n[...] = jnp.transpose(wide).astype(bf16)
    q_n[...] = jnp.transpose(q_t[...].astype(f32)).astype(bf16)


def delta_rows(high, table, given, out_t, q_t):
    slots, width, blk = given.shape
    half = slots * blk
    base = slots if high else 0
    return pl.pallas_call(
        delta_kernel,
        grid_spec=pltpu.PrefetchScalarGridSpec(
            num_scalar_prefetch=1,
            grid=(slots,),
            in_specs=[
                pl.BlockSpec((1, width, blk), lambda p, t: (t[base + p], 0, 0)),
                pl.BlockSpec((width, blk), lambda p, t: (0, p)),
                pl.BlockSpec((width, blk), lambda p, t: (0, base + p)),
            ],
            out_specs=[
                pl.BlockSpec((width, blk), lambda p, t: (0, p)),
                pl.BlockSpec((blk, width), lambda p, t: (p, 0)),
                pl.BlockSpec((1, blk), lambda p, t: (0, p)),
                pl.BlockSpec((blk, width), lambda p, t: (p, 0)),
            ],
        ),
        out_shape=[
            jax.ShapeDtypeStruct((width, half), bf16),
            jax.ShapeDtypeStruct((half, width), bf16),
            jax.ShapeDtypeStruct((1, half), f32),
            jax.ShapeDtypeStruct((half, width), bf16),
        ],
        compiler_params=pltpu.CompilerParams(vmem_limit_bytes=32 * MIB),
        name="delta_high" if high else "delta_low",
    )(table, given, out_t, q_t)


def backward_kernel(kind, base, after, *refs):
    table, q_t, q_n, grad_t, grad_n, log_total, delta, k_n, v_t = refs[:9]
    refs = refs[9:]
    cross = kind in ("first", "second")
    query_out = key_out = value_out = None
    if cross:
        (query_start, key_start, value_start), refs = refs[:3], refs[3:]
    if kind == "first":
        low_query, refs = refs[0], refs[1:]
    refs = refs[after:]
    if kind in ("high", "first"):
        query_out, refs = refs[0], refs[1:]
    elif kind == "low":
        (key_out, value_out), refs = refs[:2], refs[2:]
    out_slots, refs = refs[0], refs[1:]
    scores, grads, query_sum, key_sum, value_sum = refs
    _, tile, blk = scores.shape
    slots = out_slots.shape[0]
    width = q_t.shape[0]
    piece = blk // 2
    step = pl.program_id(0)

    @pl.when(step == 0)
    def _():
        if cross:
            query_sum[...] = query_start[...]
        else:
            query_sum[...] = jnp.zeros_like(query_sum)
        if kind == "first":
            out_slots[:, :width] = low_query[...]

    keys = k_n[...].reshape(tile, width)
    keys_t = jnp.transpose(keys.astype(f32)).astype(bf16)
    if cross:
        start = piece if kind == "second" else 0
        starts = range(start, v_t.shape[1], blk)
        values = jnp.concatenate([v_t[:, at : at + piece] for at in starts], axis=1)
    else:
        values = v_t[...]
    values = jnp.transpose(values.astype(f32)).astype(bf16)
    if cross:
        key_sum[...] = key_start[...].reshape(tile, width)
        value_sum[...] = value_start[...].reshape(tile, width)
    else:
        key_sum[...] = jnp.zeros_like(key_sum)
        value_sum[...] = jnp.zeros_like(value_sum)

    def prepare(index, slot):
        at = columns(index, blk)
        scores[slot] = dot(keys, q_t[:, at], 1, 0)
        grads[slot] = dot(values, grad_t[:, at], 1, 0)

    def absorb(index, tile_scores, prob_grads):
        at = columns(index, blk)
        rows = tile_scores.shape[0]
        probs = jnp.exp(tile_scores - log_total[:, at])
        score_grads = (probs * (prob_grads - delta[:, at])).astype(bf16)
        value_sum[:rows] += dot(probs.astype(bf16), grad_n[at, :], 1, 0)
        key_sum[:rows] += dot(score_grads, q_n[at, :], 1, 0)
        query_sum[:, at] += dot(keys_t[:, :rows], score_grads, 1, 0)

    def diagonal(half):
        index = 2 * step + half
        at = columns(index, blk)
        shape = ((half + 1) * blk, blk)
        key_pos = lax.broadcasted_iota(jnp.int32, shape, 0)
        query_pos = half * blk + lax.broadcasted_iota(jnp.int32, shape, 1)
        tile_scores = dot(keys[: shape[0]], q_t[:, at], 1, 0)
        tile_scores = jnp.where(query_pos >= key_pos, tile_scores, NEG)
        absorb(index, tile_scores, dot(values[: shape[0]], grad_t[:, at], 1, 0))

    def sweep(first, pairs):
        prepare(first, 0)

        def body(pair, carry):
            index = first + 2 * pair
            prepare(index + 1, 1)
            absorb(index, scores[0], grads[0])
            prepare(jnp.minimum(index + 2, slots - 1), 0)
            absorb(index + 1, scores[1], grads[1])
            return carry

        lax.fori_loop(0, pairs, body, 0)

    if cross:
        sweep(0, slots // 2)
    else:
        for half in range(2):
            diagonal(half)

        @pl.when(2 * step + 2 < slots)
        def _():
            sweep(2 * step + 2, slots // 2 - 1 - step)

    def query_grads(index):
        return (query_sum[:, columns(index, blk)] * 0.125).astype(bf16)

    if kind == "low":
        key_out[...] = key_sum[...]
        value_out[...] = value_sum[...]
        for half in range(2):
            index = 2 * step + half
            out_slots[table[base + index]] = query_grads(index)
    else:
        key_t = jnp.transpose(key_sum[...]).astype(bf16)
        value_t = jnp.transpose(value_sum[...]).astype(bf16)
        wide = blk if kind == "high" else piece
        for number in range(tile // wide):
            slot = table[base + tile // wide * step + number]
            part = slice(number * wide, (number + 1) * wide)
            if cross:
                out_slots[slot, width:, :piece] = key_t[:, part]
                out_slots[slot, width:, piece:] = value_t[:, part]
            else:
                out_slots[slot, :width] = key_t[:, part]
                out_slots[slot, width:] = value_t[:, part]

    @pl.when(step == pl.num_programs(0) - 1)
    def _():
        if query_out is not None:
            query_out[...] = query_sum[...]
        if kind == "second":

            def finish(index, carry):
                out_slots[table[slots + index], :width] = query_grads(index)
                return carry

            lax.fori_loop(0, slots, finish, 0)


def backward(kind, table, queries, k_n, v_t, starts, after, blk):
    width, half = queries[0].shape
    slots = half // blk
    tile = 2 * blk
    piece = blk // 2
    cross = kind in ("first", "second")
    second = 1 if kind == "second" else 0
    steps = slots // 4 if cross else slots // 2
    skip = slots // 2 if kind == "high" else 0
    if cross:
        straight = pl.BlockSpec((4, 1, piece, width), lambda i, t: (i, second, 0, 0))
        k_n = k_n.reshape(-1, 2, piece, width)
        starts = (
            (starts[0],)
            + tuple(array.reshape(-1, 2, piece, width) for array in starts[1:3])
            + tuple(starts[3:])
        )
    else:
        straight = pl.BlockSpec((tile, width), lambda i, t: (skip + i, 0))
    in_specs = [whole(array.shape) for array in queries] + [
        straight,
        pl.BlockSpec((width, 4 * blk if cross else tile), lambda i, t: (0, skip + i)),
    ]
    if cross:
        in_specs += [whole((width, half)), straight, straight]
        in_specs += [whole(array.shape) for array in starts[3:]]
    in_specs += [pl.BlockSpec(memory_space=pl.ANY)] * len(after)
    rows = width if kind == "low" else 2 * width
    held = (slots, rows, blk)
    out_specs = [whole(held)]
    out_shape = [jax.ShapeDtypeStruct(held, bf16)]
    if kind in ("high", "first"):
        out_specs = [whole((width, half))] + out_specs
        out_shape = [jax.ShapeDtypeStruct((width, half), f32)] + out_shape
    elif kind == "low":
        out_specs = [straight, straight] + out_specs
        out_shape = [jax.ShapeDtypeStruct((half, width), f32)] * 2 + out_shape
    return pl.pallas_call(
        functools.partial(backward_kernel, kind, 2 * skip, len(after)),
        grid_spec=pltpu.PrefetchScalarGridSpec(
            num_scalar_prefetch=1,
            grid=(steps,),
            in_specs=in_specs,
            out_specs=out_specs,
            scratch_shapes=[
                pltpu.VMEM((2, tile, blk), f32),
                pltpu.VMEM((2, tile, blk), f32),
                pltpu.VMEM((width, half), f32),
                pltpu.VMEM((tile, width), f32),
                pltpu.VMEM((tile, width), f32),
            ],
        ),
        out_shape=out_shape,
        compiler_params=pltpu.CompilerParams(vmem_limit_bytes=56 * MIB),
        cost_estimate=pl.CostEstimate(
            flops=4 * half * half * width,
            bytes_accessed=32 * half * width,
            transcendentals=half * half // 8,
        ),
        name="backward_" + kind,
    )(table, *queries, k_n, v_t, *starts, *after)


def weight_kernel(high_pair, first, second, a1, *refs):
    out, total, sums = refs[-3:]
    _, width, blk = second.shape
    width //= 2
    piece = blk // 2
    parts, rows, length = out.shape
    step = pl.program_id(0)

    @pl.when(step == 0)
    def _():
        total[...] = jnp.zeros_like(total)
        sums[...] = jnp.zeros_like(sums)

    low_key = jnp.concatenate([first[0, width:, :piece], second[0, width:, :piece]], axis=1)
    low_value = jnp.concatenate([first[0, width:, piece:], second[0, width:, piece:]], axis=1)
    low = jnp.concatenate([first[0, :width], low_key, low_value], axis=0)
    high = jnp.concatenate([second[0, :width], high_pair[0]], axis=0)
    total[...] += dot(low, a1[:blk], 1, 0) + dot(high, a1[blk:], 1, 0)
    wide = low.astype(f32) + high.astype(f32)
    for at in range(0, blk, 128):
        sums[...] += wide[:, at : at + 128]

    @pl.when(step == pl.num_programs(0) - 1)
    def _():
        row = jnp.sum(jnp.transpose(sums[...]), axis=0, keepdims=True)
        tail = [row[:, number * width : (number + 1) * width] for number in range(3)]
        tail = jnp.concatenate(tail, axis=0)
        tail = jnp.concatenate([tail, jnp.zeros((3, length - width), f32)], axis=1)
        tail = jnp.concatenate([tail, jnp.zeros((rows - 3 * width - 3, length), f32)], axis=0)
        for part in range(parts):
            own = total[:, part * length : (part + 1) * length]
            out[part] = jnp.concatenate([own, tail], axis=0).astype(bf16)


def weight_grad(high_pair, first, second, a1_full, parts, after):
    slots, width, blk = second.shape
    width //= 2
    tokens, model = a1_full.shape
    rows = 3 * width
    shape = (parts, rows + 16, model // parts)
    given = (high_pair, first, second)
    return pl.pallas_call(
        weight_kernel,
        grid=(slots,),
        in_specs=[pl.BlockSpec((1,) + array.shape[1:], lambda s: (s, 0, 0)) for array in given]
        + [pl.BlockSpec((2 * blk, model), lambda s: (s, 0))]
        + [pl.BlockSpec(memory_space=pl.ANY)] * len(after),
        out_specs=whole(shape),
        out_shape=jax.ShapeDtypeStruct(shape, bf16),
        scratch_shapes=[pltpu.VMEM((rows, model), f32), pltpu.VMEM((rows, 128), f32)],
        compiler_params=pltpu.CompilerParams(vmem_limit_bytes=48 * MIB),
        cost_estimate=pl.CostEstimate(
            flops=2 * rows * tokens * model, bytes_accessed=2 * tokens * model, transcendentals=0
        ),
        name="weight_grad",
    )(*given, a1_full, *after)


def mlp_forward_kernel(normed, up, up_bias, down, hidden, slope, total):
    @pl.when(pl.program_id(0) == 0)
    def _():
        total[...] = jnp.zeros_like(total)

    value, bend = gelu_and_slope(dot(normed[...], up[...], 1, 1) + up_bias[...])
    low = value.astype(bf16)
    hidden[...] = low
    slope[...] = bend.astype(bf16)
    total[...] += dot(low, down[...], 1, 0)


def mlp_backward_kernel(grad, down, slope, up, grad_pre, sums, total):
    @pl.when(pl.program_id(0) == 0)
    def _():
        total[...] = jnp.zeros_like(total)

    low = (dot(grad[...], down[...], 1, 1) * slope[...].astype(f32)).astype(bf16)
    grad_pre[...] = low
    sums[...] = jnp.sum(low.astype(f32), axis=0, keepdims=True)
    total[...] += dot(low, up[...], 1, 0)


def mlp_grads_kernel(hidden, grad, grad_pre, normed, down_out, up_out):
    down_out[...] = dot(hidden[...], grad[...], 0, 0).astype(bf16)
    up_out[...] = dot(grad_pre[...], normed[...], 0, 0).astype(bf16)


def mlp_call(kernel, name, operands, kinds, results, result_kinds, rows, model, hidden):
    chunk = 512
    specs = {
        "rows": whole((rows, model)),
        "wide": pl.BlockSpec((rows, chunk), lambda j: (0, j)),
        "tall": pl.BlockSpec((chunk, model), lambda j: (j, 0)),
        "line": pl.BlockSpec((1, chunk), lambda j: (0, j)),
    }
    shapes = {
        "rows": (rows, model),
        "wide": (rows, hidden),
        "tall": (hidden, model),
        "line": (1, hidden),
    }
    return pl.pallas_call(
        kernel,
        grid=(hidden // chunk,),
        in_specs=[specs[kind] for kind in kinds],
        out_specs=[specs[kind] for kind in result_kinds],
        out_shape=[
            jax.ShapeDtypeStruct(shapes[kind], dtype) for kind, dtype in zip(result_kinds, results)
        ],
        compiler_params=pltpu.CompilerParams(vmem_limit_bytes=56 * MIB),
        cost_estimate=pl.CostEstimate(
            flops=4 * rows * model * hidden, bytes_accessed=8 * rows * hidden, transcendentals=0
        ),
        name=name,
    )(*operands)


def place_kernel(given, out):
    count, width, length = given.shape
    out[...] = jnp.transpose(given[...].reshape(count * width, length)).astype(f32)


def place(gathered, width):
    heads, _, length = gathered.shape
    count = 4
    groups = heads // count
    return pl.pallas_call(
        place_kernel,
        grid=(3, groups),
        in_specs=[pl.BlockSpec((count, width, length), lambda c, i: (i, c, 0))],
        out_specs=pl.BlockSpec((length, count * width), lambda c, i: (0, c * groups + i)),
        out_shape=jax.ShapeDtypeStruct((length, 3 * heads * width), f32),
        compiler_params=pltpu.CompilerParams(vmem_limit_bytes=32 * MIB),
        name="place",
    )(gathered)


def local(
    groups,
    activations,
    block_order,
    qkv_weight,
    qv_bias,
    proj_weight,
    proj_bias,
    up_weight,
    up_bias,
    down_weight,
    down_bias,
    norm_gains,
    norm_biases,
    cotangent,
):
    _, rows, model = activations.shape
    blk = rows // 2
    width = model // HEADS
    ctx = ("r", "h")
    everywhere = ("r", "h", "wt")
    devices = groups * HEADS
    weight_parts = lax.axis_size("wt")
    head = lax.axis_index("h")
    group = lax.axis_index("r")
    part = lax.axis_index("wt")

    small = (qv_bias, proj_bias, up_bias, down_bias, norm_gains, norm_biases)
    packed = jnp.concatenate([array.reshape(-1) for array in small])
    gathered = lax.all_gather(packed, "wt", axis=0)
    pieces, start = [], 0
    for array in small:
        piece = gathered[:, start : start + array.size].reshape((weight_parts,) + array.shape)
        start += array.size
        if array.ndim == 2:
            piece = jnp.transpose(piece, (1, 0, 2)).reshape(array.shape[0], -1)
        else:
            piece = piece.reshape(-1)
        pieces.append(piece.astype(f32))
    qvbias, projbias, upbias, downbias, gains, shifts = pieces

    inputs = activations.reshape(rows, model).astype(f32)
    upstream = cotangent.reshape(rows, model).astype(f32)
    a1 = layer_norm(inputs, gains[0], shifts[0]).astype(bf16)
    a1_full = lax.all_gather(a1, ctx, axis=0, tiled=True)

    mine = lax.dynamic_index_in_dim(
        qkv_weight.reshape(-1, 3, HEADS, width), head, axis=2, keepdims=False
    )
    mine = lax.all_gather(mine.reshape(-1, 3 * width), "wt", axis=0, tiled=True)
    scale = 1.0 / math.sqrt(width)
    mine = jnp.concatenate(
        [mine[:, :width] * bf16(scale), mine[:, 2 * width :], mine[:, width : 2 * width]], axis=1
    )
    q_bias = lax.dynamic_slice(qvbias, (head * width,), (width,))
    v_bias = lax.dynamic_slice(qvbias, (model + head * width,), (width,))
    bias = jnp.concatenate([q_bias * scale, v_bias, jnp.zeros_like(q_bias)])

    lows = block_order.reshape(devices, 2)[:, 0]
    numbers = jnp.arange(devices, dtype=jnp.int32)
    owner = jnp.sum(jnp.where(lows[None, :] == numbers[:, None], numbers[None, :], 0), axis=1)
    owner = jnp.concatenate([owner, owner[::-1]]).astype(jnp.int32)
    is_high = (jnp.arange(2 * devices, dtype=jnp.int32) >= devices).astype(jnp.int32)
    slot_of = 2 * owner + is_high

    half = devices * blk
    q_t, k_n, v_t = project(slot_of, a1_full, mine, bias[None, :], blk, width)
    out_low, log_low, slots_low = forward(False, owner, q_t, k_n, v_t, blk)
    out_high, log_high, slots_high = forward(True, owner, q_t, k_n, v_t, blk)

    def to_tokens(array):
        own = lax.dynamic_slice_in_dim(array, group * HEADS, HEADS, 0)
        return lax.all_to_all(own, "h", 0, 0, tiled=True).reshape(-1, blk)

    def to_heads(array):
        array = lax.all_to_all(array.reshape(HEADS, width, blk), "h", 0, 0, tiled=True)
        if groups > 1:
            array = lax.all_gather(array, "r", axis=0, tiled=True)
        return array

    attended_t = jnp.concatenate([to_tokens(slots_low), to_tokens(slots_high)], axis=1)

    full_proj = lax.all_gather(proj_weight, "wt", axis=0, tiled=True)
    up_full = lax.all_gather(up_weight, "wt", axis=0, tiled=True)
    down_full = lax.all_gather(down_weight, "wt", axis=0, tiled=True)
    full_qkv = lax.all_gather(qkv_weight, "wt", axis=0, tiled=True)

    proj_pre = dot(attended_t, full_proj, 0, 0) + projbias
    residual = inputs + layer_norm(proj_pre, gains[1], shifts[1])
    normed_mid = layer_norm(residual, gains[2], shifts[2]).astype(bf16)
    sizes = (rows, model, up_full.shape[0])
    hidden, slope, branch = mlp_call(
        mlp_forward_kernel,
        "mlp_forward",
        (normed_mid, up_full, upbias[None, :], down_full),
        ("rows", "tall", "line", "tall"),
        (bf16, bf16, f32),
        ("wide", "wide", "rows"),
        *sizes,
    )
    branch = branch + downbias
    layer_output = (residual + layer_norm(branch, gains[3], shifts[3])).astype(bf16)

    grad_branch, gain_three, shift_three = norm_backward(branch, gains[3], shifts[3], upstream)
    grad_branch = grad_branch.astype(bf16)
    grad_pre, up_sums, grad_mid = mlp_call(
        mlp_backward_kernel,
        "mlp_backward",
        (grad_branch, down_full, slope, up_full),
        ("rows", "tall", "wide", "tall"),
        (bf16, f32, f32),
        ("wide", "line", "rows"),
        *sizes,
    )
    grad_residual, gain_two, shift_two = norm_backward(residual, gains[2], shifts[2], grad_mid)
    grad_residual = upstream + grad_residual
    grad_proj_pre, gain_one, shift_one = norm_backward(
        proj_pre, gains[1], shifts[1], grad_residual
    )
    grad_proj_pre = grad_proj_pre.astype(bf16)
    grad_attended_t = dot(full_proj, grad_proj_pre, 1, 1).astype(bf16)
    given_high = to_heads(grad_attended_t[:, blk:])
    given_low = to_heads(grad_attended_t[:, :blk])

    grad_downward, grad_upward = mlp_call(
        mlp_grads_kernel,
        "mlp_grads",
        (hidden, grad_branch, grad_pre, normed_mid),
        ("wide", "rows", "wide", "rows"),
        (bf16, bf16),
        ("tall", "tall"),
        *sizes,
    )
    grad_proj = dot(attended_t, grad_proj_pre, 1, 0).astype(bf16)

    def own_rows(array):
        length = array.shape[0] // weight_parts
        return lax.dynamic_slice_in_dim(array, part * length, length, 0)

    early = jnp.concatenate(
        [
            up_sums[0],
            jnp.sum(grad_branch.astype(f32), axis=0),
            jnp.sum(grad_proj_pre.astype(f32), axis=0),
            gain_one,
            gain_two,
            gain_three,
            shift_one,
            shift_two,
            shift_three,
        ]
    ).astype(bf16)
    grad_proj = jnp.concatenate([grad_proj, early.reshape(-1, model)], axis=0)
    given_high, grad_downward, grad_upward, grad_proj = lax.optimization_barrier(
        (given_high, grad_downward, grad_upward, grad_proj)
    )
    summed = lax.psum((grad_downward, grad_upward, grad_proj), everywhere)
    grad_downward, grad_upward, grad_proj = summed
    early = grad_proj[model:].astype(f32).reshape(-1)
    grad_proj = grad_proj[:model]
    grad_downward = own_rows(grad_downward).astype(f32)
    grad_upward = own_rows(grad_upward).astype(f32)
    grad_proj = own_rows(grad_proj).astype(f32)
    hidden_width = up_full.shape[0]
    grad_upbias = own_rows(early[:hidden_width])
    early = early[hidden_width:].reshape(8, model)
    grad_downbias = own_rows(early[0])
    grad_projbias = own_rows(early[1])

    def token_grads(array):
        own = lax.dynamic_slice_in_dim(array, group * HEADS, HEADS, 0)
        own = lax.all_to_all(own, "h", 0, 0, tiled=True)
        own = own.reshape(HEADS, -1, width, array.shape[2])
        return jnp.transpose(own, (1, 0, 2, 3)).reshape(-1, array.shape[2])

    grad_t, grad_n, delta, q_n = delta_rows(True, owner, given_high, out_high, q_t)
    high = (q_t[:, half:], q_n, grad_t, grad_n, log_high, delta)
    query_sum, high_pair = backward("high", owner, high, k_n, v_t, (), (), blk)
    high_tokens = token_grads(high_pair)
    grad_t, grad_n, delta, q_n = delta_rows(False, owner, given_low, out_low, q_t)
    low = (q_t[:, :half], q_n, grad_t, grad_n, log_low, delta)
    key_sum, value_sum, low_query = backward("low", owner, low, k_n, v_t, (), (), blk)
    starts = (query_sum, key_sum, value_sum, low_query)
    query_sum, first = backward("first", owner, high, k_n, v_t, starts, (high_tokens,), blk)
    first_tokens = token_grads(first)
    starts = (query_sum, key_sum, value_sum)
    (second,) = backward("second", owner, high, k_n, v_t, starts, (), blk)
    second_tokens = token_grads(second)

    def own_columns(array):
        length = array.shape[1] // weight_parts
        return lax.dynamic_slice_in_dim(array, part * length, length, 1)

    after = (first_tokens,) + tuple(summed)
    columns_grad = weight_grad(high_pair, first, second, a1_full, weight_parts, after)
    columns_grad = lax.all_to_all(columns_grad, "wt", 0, 0, tiled=True)
    columns_grad = jnp.sum(columns_grad.astype(f32), axis=0).astype(bf16)
    all_columns = lax.all_gather(columns_grad, "h", axis=0)
    grad_qkv = place(all_columns, width)
    sums = all_columns[:, 3 * width : 3 * width + 3, :width].astype(f32)
    sums = jnp.transpose(sums, (1, 0, 2)).reshape(3, model)
    grad_qvbias = own_rows(jnp.concatenate([sums[0], sums[2]]))

    own_weight = qkv_weight.astype(f32)
    shift_zero = jnp.sum(own_weight * sums.reshape(1, -1), axis=1)
    gain_zero = jnp.sum(own_weight * grad_qkv, axis=1)
    first_norm = own_columns(jnp.stack([gains[0], shifts[0]]))
    gain_zero = (gain_zero - first_norm[1] * shift_zero) / first_norm[0]

    second_tokens, grad_downward, grad_upward, grad_proj = lax.optimization_barrier(
        (second_tokens, grad_downward, grad_upward, grad_proj)
    )
    piece = blk // 2
    low_key = [first_tokens[model:, :piece], second_tokens[model:, :piece]]
    low_value = [first_tokens[model:, piece:], second_tokens[model:, piece:]]
    low_rows = [
        first_tokens[:model],
        jnp.concatenate(low_key, axis=1),
        jnp.concatenate(low_value, axis=1),
    ]
    high_rows = [second_tokens[:model], high_tokens]
    grads_t = jnp.concatenate(
        [jnp.concatenate(low_rows, axis=0), jnp.concatenate(high_rows, axis=0)], axis=1
    )
    grad_normed = dot(grads_t, full_qkv, 0, 1)
    grad_inputs, _, _ = norm_backward(inputs, gains[0], shifts[0], grad_normed)
    input_grad = (grad_residual + grad_inputs).reshape(1, rows, model)
    early = own_columns(early)
    grad_gains = jnp.concatenate([gain_zero[None], early[2:5]], axis=0)
    grad_biases = jnp.concatenate([shift_zero[None], early[5:8]], axis=0)
    return (
        layer_output.reshape(1, rows, model),
        input_grad,
        grad_qkv,
        grad_qvbias,
        grad_proj,
        grad_projbias,
        grad_upward,
        grad_upbias,
        grad_downward,
        grad_downbias,
        grad_gains,
        grad_biases,
    )


def solution(mesh):
    groups = mesh.shape["ctx"] // HEADS
    split = Mesh(
        mesh.devices.reshape(groups, HEADS, mesh.shape["wt"]), ("r", "h", "wt")
    )
    tokens = P("wt", ("r", "h"), None)
    rows, flat, cols = P("wt", None), P("wt"), P(None, "wt")
    return jax.shard_map(
        functools.partial(local, groups),
        mesh=split,
        in_specs=(tokens, P(), rows, flat, rows, flat, rows, flat, rows, flat, cols, cols, tokens),
        out_specs=(tokens, tokens, rows, flat, rows, flat, rows, flat, rows, flat, cols, cols),
        check_vma=False,
    )
```

```python
import functools
import math

import jax
import jax.numpy as jnp
from jax import lax
from jax.experimental import pallas as pl
from jax.experimental.pallas import tpu as pltpu
from jax.sharding import Mesh
from jax.sharding import PartitionSpec as P

HEADS = 16
ALPHA = 32.0
EPS = 1e-05
NEG = -1e30
bf16 = jnp.bfloat16
f32 = jnp.float32
MIB = 1 << 20


def layer_norm(values, norm_gain, norm_shift):
    average = jnp.mean(values, axis=-1, keepdims=True)
    centered = values - average
    variance = jnp.mean(centered * centered, axis=-1, keepdims=True)
    return centered * lax.rsqrt(variance + EPS) * norm_gain + norm_shift


def norm_backward(values, norm_gain, norm_shift, upstream):
    _, pullback = jax.vjp(layer_norm, values, norm_gain, norm_shift)
    return pullback(upstream)


def gelu_and_slope(values):
    squared = values * values
    scale = math.sqrt(2.0 / math.pi)
    bent = jnp.tanh(scale * (values * (1.0 + 0.044715 * squared)))
    half = 0.5 * (1.0 + bent)
    slope = half + (0.5 * scale) * values * (1.0 - bent * bent) * (1.0 + 0.134145 * squared)
    return values * half, slope


def dot(a, b, ca, cb):
    return lax.dot_general(a, b, (((ca,), (cb,)), ((), ())), preferred_element_type=f32)


def columns(index, width):
    return pl.ds(pl.multiple_of(index * width, width), width)


def whole(shape):
    return pl.BlockSpec(shape, lambda *_: (0,) * len(shape), pipeline_mode=pl.Buffered(1))


def project_kernel(table, *refs):
    blocks, (weight, bias, q_t, k_n, v_t) = refs[:-5], refs[-5:]
    width = k_n.shape[1]
    for number, rows in enumerate(blocks):
        blk = rows.shape[0]
        part = slice(number * blk, (number + 1) * blk)
        heads = (dot(rows[...], weight[...], 1, 0) + bias[...]).astype(bf16)
        turned = jnp.transpose(heads[:, : 2 * width])
        q_t[:, part] = turned[:width]
        v_t[:, part] = turned[width:]
        k_n[part, :] = heads[:, 2 * width :]


def project(table, a1_full, weight, bias, blk, width):
    tokens, model = a1_full.shape
    count = 4
    tile = count * blk
    turned = pl.BlockSpec((width, tile), lambda i, t: (0, i))
    straight = pl.BlockSpec((tile, width), lambda i, t: (i, 0))

    def block(number):
        return pl.BlockSpec((blk, model), lambda i, t: (t[count * i + number], 0))

    return pl.pallas_call(
        project_kernel,
        grid_spec=pltpu.PrefetchScalarGridSpec(
            num_scalar_prefetch=1,
            grid=(tokens // tile,),
            in_specs=[block(number) for number in range(count)]
            + [whole(weight.shape), whole(bias.shape)],
            out_specs=[turned, straight, turned],
        ),
        out_shape=[
            jax.ShapeDtypeStruct((width, tokens), bf16),
            jax.ShapeDtypeStruct((tokens, width), bf16),
            jax.ShapeDtypeStruct((width, tokens), bf16),
        ],
        compiler_params=pltpu.CompilerParams(vmem_limit_bytes=48 * MIB),
        cost_estimate=pl.CostEstimate(
            flops=8 * tokens * model * width, bytes_accessed=2 * tokens * model, transcendentals=0
        ),
        name="project",
    )(table, *([a1_full] * count), weight, bias)


def forward_kernel(base, table, q_t, k_n, v_t, out_t, log_total, out_slots, scores):
    _, width, blk = out_slots.shape
    tile = q_t.shape[1]
    step = base + pl.program_id(0)
    query = q_t[...]

    def score(index):
        return dot(k_n[columns(index, blk), :], query, 1, 0)

    def prepare(index, slot):
        tile_scores = score(index)
        scores[slot] = tile_scores
        return jnp.max(tile_scores, axis=0, keepdims=True)

    ones = jnp.ones((16, blk), bf16)

    def absorb(index, tile_scores, peak, summed, tile_peak):
        new_peak = jnp.maximum(peak, tile_peak)
        weights = jnp.exp(tile_scores - new_peak).astype(bf16)
        keep = jnp.exp(peak - new_peak)
        values = jnp.concatenate([v_t[:, columns(index, blk)], ones], axis=0)
        return new_peak, summed * keep + dot(values, weights, 1, 0)

    def body(pair, carry):
        peak, summed, tile_peak = carry
        for slot in range(2):
            next_peak = prepare(2 * pair + slot + 1, 1 - slot)
            peak, summed = absorb(2 * pair + slot, scores[slot], peak, summed, tile_peak)
            tile_peak = next_peak
        return peak, summed, tile_peak

    carry = (
        jnp.full((1, tile), -jnp.inf, f32),
        jnp.zeros((width + 16, tile), f32),
        prepare(0, 0),
    )
    peak, summed, _ = lax.fori_loop(0, step, body, carry)
    for half in range(2):
        part = query[:, half * blk :]
        shape = (blk, tile - half * blk)
        key_pos = lax.broadcasted_iota(jnp.int32, shape, 0)
        query_pos = lax.broadcasted_iota(jnp.int32, shape, 1)
        tile_scores = dot(k_n[columns(2 * step + half, blk), :], part, 1, 0)
        tile_scores = jnp.where(query_pos >= key_pos, tile_scores, NEG)
        tile_peak = jnp.max(tile_scores, axis=0, keepdims=True)
        state = absorb(2 * step + half, tile_scores, peak, summed, tile_peak)
        if half == 0:
            left = tuple(array[:, :blk] for array in state)
            peak, summed = (array[:, blk:] for array in state)
    peak, summed = (
        jnp.concatenate([first, second], axis=1) for first, second in zip(left, state)
    )
    total = summed[width : width + 1]
    result = summed[:width] / total
    out_t[...] = result
    log_total[...] = peak + jnp.log(total)
    low = result.astype(bf16)
    for half in range(2):
        out_slots[table[2 * step + half]] = low[:, half * blk : (half + 1) * blk]


def forward(high, table, q_t, k_n, v_t, blk):
    width, tokens = q_t.shape
    slots = tokens // (2 * blk)
    tile = 2 * blk
    steps = slots // 2
    base = steps if high else 0
    seen = tokens if high else tokens // 2
    return pl.pallas_call(
        functools.partial(forward_kernel, base),
        grid_spec=pltpu.PrefetchScalarGridSpec(
            num_scalar_prefetch=1,
            grid=(steps,),
            in_specs=[
                pl.BlockSpec((width, tile), lambda i, t: (0, base + i)),
                whole((seen, width)),
                whole((width, seen)),
            ],
            out_specs=[
                pl.BlockSpec((width, tile), lambda i, t: (0, i)),
                pl.BlockSpec((1, tile), lambda i, t: (0, i)),
                whole((slots, width, blk)),
            ],
            scratch_shapes=[pltpu.VMEM((2, blk, tile), f32)],
        ),
        out_shape=[
            jax.ShapeDtypeStruct((width, tokens // 2), f32),
            jax.ShapeDtypeStruct((1, tokens // 2), f32),
            jax.ShapeDtypeStruct((slots, width, blk), bf16),
        ],
        compiler_params=pltpu.CompilerParams(vmem_limit_bytes=56 * MIB),
        cost_estimate=pl.CostEstimate(
            flops=(6 if high else 2) * tokens * tokens * width,
            bytes_accessed=12 * tokens * width,
            transcendentals=(3 if high else 1) * tokens * tokens // 8,
        ),
        name="forward_high" if high else "forward_low",
    )(table, q_t, k_n, v_t)


def delta_kernel(table, given, out_t, q_t, grad_t, grad_n, delta, q_n):
    block = given[0]
    grad_t[...] = block
    wide = block.astype(f32)
    delta[...] = jnp.sum(wide * out_t[...], axis=0, keepdims=True)
    grad_n[...] = jnp.transpose(wide).astype(bf16)
    q_n[...] = jnp.transpose(q_t[...].astype(f32)).astype(bf16)


def delta_rows(high, table, given, out_t, q_t):
    slots, width, blk = given.shape
    half = slots * blk
    base = slots if high else 0
    return pl.pallas_call(
        delta_kernel,
        grid_spec=pltpu.PrefetchScalarGridSpec(
            num_scalar_prefetch=1,
            grid=(slots,),
            in_specs=[
                pl.BlockSpec((1, width, blk), lambda p, t: (t[base + p], 0, 0)),
                pl.BlockSpec((width, blk), lambda p, t: (0, p)),
                pl.BlockSpec((width, blk), lambda p, t: (0, base + p)),
            ],
            out_specs=[
                pl.BlockSpec((width, blk), lambda p, t: (0, p)),
                pl.BlockSpec((blk, width), lambda p, t: (p, 0)),
                pl.BlockSpec((1, blk), lambda p, t: (0, p)),
                pl.BlockSpec((blk, width), lambda p, t: (p, 0)),
            ],
        ),
        out_shape=[
            jax.ShapeDtypeStruct((width, half), bf16),
            jax.ShapeDtypeStruct((half, width), bf16),
            jax.ShapeDtypeStruct((1, half), f32),
            jax.ShapeDtypeStruct((half, width), bf16),
        ],
        compiler_params=pltpu.CompilerParams(vmem_limit_bytes=32 * MIB),
        name="delta_high" if high else "delta_low",
    )(table, given, out_t, q_t)


def backward_kernel(kind, base, after, *refs):
    table, q_t, q_n, grad_t, grad_n, log_total, delta, k_n, v_t = refs[:9]
    refs = refs[9:]
    cross = kind in ("first", "second")
    query_out = key_out = value_out = None
    if cross:
        (query_start, key_start, value_start), refs = refs[:3], refs[3:]
    if kind == "first":
        low_query, refs = refs[0], refs[1:]
    refs = refs[after:]
    if kind == "second":
        query_slots, refs = refs[0], refs[1:]
    if kind in ("high", "first"):
        query_out, refs = refs[0], refs[1:]
    elif kind == "low":
        (key_out, value_out), refs = refs[:2], refs[2:]
    out_slots, refs = refs[0], refs[1:]
    scores, grads, query_sum, key_sum, value_sum = refs
    _, tile, blk = scores.shape
    slots = out_slots.shape[0]
    width = q_t.shape[0]
    piece = blk // 2
    step = pl.program_id(0)

    @pl.when(step == 0)
    def _():
        if cross:
            query_sum[...] = query_start[...]
        else:
            query_sum[...] = jnp.zeros_like(query_sum)
        if kind == "first":
            out_slots[:, :width] = low_query[...]

    keys = k_n[...].reshape(tile, width)
    keys_t = jnp.transpose(keys.astype(f32)).astype(bf16)
    if cross:
        start = piece if kind == "second" else 0
        starts = range(start, v_t.shape[1], blk)
        values = jnp.concatenate([v_t[:, at : at + piece] for at in starts], axis=1)
    else:
        values = v_t[...]
    values = jnp.transpose(values.astype(f32)).astype(bf16)
    if cross:
        key_sum[...] = key_start[...].reshape(tile, width)
        value_sum[...] = value_start[...].reshape(tile, width)
    else:
        key_sum[...] = jnp.zeros_like(key_sum)
        value_sum[...] = jnp.zeros_like(value_sum)

    def prepare(index, slot):
        at = columns(index, blk)
        scores[slot] = dot(keys, q_t[:, at], 1, 0)
        grads[slot] = dot(values, grad_t[:, at], 1, 0)

    def absorb(index, tile_scores, prob_grads):
        at = columns(index, blk)
        rows = tile_scores.shape[0]
        probs = jnp.exp(tile_scores - log_total[:, at])
        score_grads = (probs * (prob_grads - delta[:, at])).astype(bf16)
        value_sum[:rows] += dot(probs.astype(bf16), grad_n[at, :], 1, 0)
        key_sum[:rows] += dot(score_grads, q_n[at, :], 1, 0)
        query_sum[:, at] += dot(keys_t[:, :rows], score_grads, 1, 0)

    def diagonal(half):
        index = 2 * step + half
        at = columns(index, blk)
        shape = ((half + 1) * blk, blk)
        key_pos = lax.broadcasted_iota(jnp.int32, shape, 0)
        query_pos = half * blk + lax.broadcasted_iota(jnp.int32, shape, 1)
        tile_scores = dot(keys[: shape[0]], q_t[:, at], 1, 0)
        tile_scores = jnp.where(query_pos >= key_pos, tile_scores, NEG)
        absorb(index, tile_scores, dot(values[: shape[0]], grad_t[:, at], 1, 0))

    def sweep(first, pairs):
        prepare(first, 0)

        def body(pair, carry):
            index = first + 2 * pair
            prepare(index + 1, 1)
            absorb(index, scores[0], grads[0])
            prepare(jnp.minimum(index + 2, slots - 1), 0)
            absorb(index + 1, scores[1], grads[1])
            return carry

        lax.fori_loop(0, pairs, body, 0)

    if cross:
        sweep(0, slots // 2)
    else:
        for half in range(2):
            diagonal(half)

        @pl.when(2 * step + 2 < slots)
        def _():
            sweep(2 * step + 2, slots // 2 - 1 - step)

    def query_grads(index):
        return (query_sum[:, columns(index, blk)] * 0.125).astype(bf16)

    if kind == "low":
        key_out[...] = key_sum[...]
        value_out[...] = value_sum[...]
        for half in range(2):
            index = 2 * step + half
            out_slots[table[base + index]] = query_grads(index)
    else:
        key_t = jnp.transpose(key_sum[...]).astype(bf16)
        value_t = jnp.transpose(value_sum[...]).astype(bf16)
        wide = blk if kind == "high" else piece
        for number in range(tile // wide):
            slot = table[base + tile // wide * step + number]
            part = slice(number * wide, (number + 1) * wide)
            if kind == "first":
                out_slots[slot, width:, :piece] = key_t[:, part]
                out_slots[slot, width:, piece:] = value_t[:, part]
            else:
                out_slots[slot, :width] = key_t[:, part]
                out_slots[slot, width:] = value_t[:, part]

    @pl.when(step == pl.num_programs(0) - 1)
    def _():
        if query_out is not None:
            query_out[...] = query_sum[...]
        if kind == "second":

            def finish(index, carry):
                query_slots[table[slots + index]] = query_grads(index)
                return carry

            lax.fori_loop(0, slots, finish, 0)


def backward(kind, table, queries, k_n, v_t, starts, after, blk):
    width, half = queries[0].shape
    slots = half // blk
    tile = 2 * blk
    piece = blk // 2
    cross = kind in ("first", "second")
    second = 1 if kind == "second" else 0
    steps = slots // 4 if cross else slots // 2
    skip = slots // 2 if kind == "high" else 0
    if cross:
        straight = pl.BlockSpec((4, 1, piece, width), lambda i, t: (i, second, 0, 0))
        k_n = k_n.reshape(-1, 2, piece, width)
        starts = (
            (starts[0],)
            + tuple(array.reshape(-1, 2, piece, width) for array in starts[1:3])
            + tuple(starts[3:])
        )
    else:
        straight = pl.BlockSpec((tile, width), lambda i, t: (skip + i, 0))
    in_specs = [whole(array.shape) for array in queries] + [
        straight,
        pl.BlockSpec((width, 4 * blk if cross else tile), lambda i, t: (0, skip + i)),
    ]
    if cross:
        in_specs += [whole((width, half)), straight, straight]
        in_specs += [whole(array.shape) for array in starts[3:]]
    in_specs += [pl.BlockSpec(memory_space=pl.ANY)] * len(after)
    rows = width if kind == "low" else 2 * width
    held = (slots, rows, piece if kind == "second" else blk)
    out_specs = [whole(held)]
    out_shape = [jax.ShapeDtypeStruct(held, bf16)]
    if kind in ("high", "first"):
        out_specs = [whole((width, half))] + out_specs
        out_shape = [jax.ShapeDtypeStruct((width, half), f32)] + out_shape
    elif kind == "second":
        out_specs = [whole((slots, width, blk))] + out_specs
        out_shape = [jax.ShapeDtypeStruct((slots, width, blk), bf16)] + out_shape
    elif kind == "low":
        out_specs = [straight, straight] + out_specs
        out_shape = [jax.ShapeDtypeStruct((half, width), f32)] * 2 + out_shape
    return pl.pallas_call(
        functools.partial(backward_kernel, kind, 2 * skip, len(after)),
        grid_spec=pltpu.PrefetchScalarGridSpec(
            num_scalar_prefetch=1,
            grid=(steps,),
            in_specs=in_specs,
            out_specs=out_specs,
            scratch_shapes=[
                pltpu.VMEM((2, tile, blk), f32),
                pltpu.VMEM((2, tile, blk), f32),
                pltpu.VMEM((width, half), f32),
                pltpu.VMEM((tile, width), f32),
                pltpu.VMEM((tile, width), f32),
            ],
        ),
        out_shape=out_shape,
        compiler_params=pltpu.CompilerParams(vmem_limit_bytes=56 * MIB),
        cost_estimate=pl.CostEstimate(
            flops=4 * half * half * width,
            bytes_accessed=32 * half * width,
            transcendentals=half * half // 8,
        ),
        name="backward_" + kind,
    )(table, *queries, k_n, v_t, *starts, *after)


def weight_kernel(part, high_pair, first, query, second, a1, down, up, *refs):
    out, down_out, up_out, total, sums = refs[-5:]
    _, width, blk = query.shape
    down_out[...] = down[...].astype(f32)
    up_out[...] = up[...].astype(f32)
    piece = blk // 2
    parts, rows, length = out.shape
    step = pl.program_id(0)

    @pl.when(step == 0)
    def _():
        total[...] = jnp.zeros_like(total)
        sums[...] = jnp.zeros_like(sums)

    low_key = jnp.concatenate([first[0, width:, :piece], second[0, :width]], axis=1)
    low_value = jnp.concatenate([first[0, width:, piece:], second[0, width:]], axis=1)
    low = jnp.concatenate([first[0, :width], low_key, low_value], axis=0)
    high = jnp.concatenate([query[0], high_pair[0]], axis=0)
    total[...] += dot(low, a1[:blk], 1, 0) + dot(high, a1[blk:], 1, 0)
    wide = low.astype(f32) + high.astype(f32)
    for at in range(0, blk, 128):
        sums[...] += wide[:, at : at + 128]

    @pl.when(step == pl.num_programs(0) - 1)
    def _():
        row = jnp.sum(jnp.transpose(sums[...]), axis=0, keepdims=True)
        tail = [row[:, number * width : (number + 1) * width] for number in range(3)]
        tail = jnp.concatenate(tail, axis=0)
        tail = jnp.concatenate([tail, jnp.zeros((3, length - width), f32)], axis=1)
        tail = jnp.concatenate([tail, jnp.zeros((rows - 3 * width - 3, length), f32)], axis=0)
        for number in range(parts):
            own = total[:, number * length : (number + 1) * length]
            out[number] = jnp.concatenate([own, tail], axis=0).astype(bf16)


def weight_grad(part, high_pair, first, query, second, a1_full, down, up, parts, after):
    slots, width, blk = query.shape
    tokens, model = a1_full.shape
    rows = 3 * width
    shape = (parts, rows + 16, model // parts)
    given = (high_pair, first, query, second)
    own = down.shape[0] // parts
    strip = own // slots
    summed = pl.BlockSpec((strip, model), lambda s, t: (t[0] * slots + s, 0))
    kept = pl.BlockSpec((strip, model), lambda s, t: (s, 0))
    return pl.pallas_call(
        weight_kernel,
        grid_spec=pltpu.PrefetchScalarGridSpec(
            num_scalar_prefetch=1,
            grid=(slots,),
            in_specs=[
                pl.BlockSpec((1,) + array.shape[1:], lambda s, t: (s, 0, 0)) for array in given
            ]
            + [pl.BlockSpec((2 * blk, model), lambda s, t: (s, 0)), summed, summed]
            + [pl.BlockSpec(memory_space=pl.ANY)] * len(after),
            out_specs=[whole(shape), kept, kept],
            scratch_shapes=[pltpu.VMEM((rows, model), f32), pltpu.VMEM((rows, 128), f32)],
        ),
        out_shape=[jax.ShapeDtypeStruct(shape, bf16)]
        + [jax.ShapeDtypeStruct((own, model), f32)] * 2,
        compiler_params=pltpu.CompilerParams(vmem_limit_bytes=48 * MIB),
        cost_estimate=pl.CostEstimate(
            flops=2 * rows * tokens * model, bytes_accessed=2 * tokens * model, transcendentals=0
        ),
        name="weight_grad",
    )(part.reshape(1), *given, a1_full, down, up, *after)


def mlp_forward_kernel(normed, up, up_bias, down, hidden, slope, total):
    @pl.when(pl.program_id(0) == 0)
    def _():
        total[...] = jnp.zeros_like(total)

    value, bend = gelu_and_slope(dot(normed[...], up[...], 1, 1) + up_bias[...])
    low = value.astype(bf16)
    hidden[...] = low
    slope[...] = bend.astype(bf16)
    total[...] += dot(low, down[...], 1, 0)


def mlp_backward_kernel(grad, down, slope, up, grad_pre, sums, total):
    @pl.when(pl.program_id(0) == 0)
    def _():
        total[...] = jnp.zeros_like(total)

    low = (dot(grad[...], down[...], 1, 1) * slope[...].astype(f32)).astype(bf16)
    grad_pre[...] = low
    sums[...] = jnp.sum(low.astype(f32), axis=0, keepdims=True)
    total[...] += dot(low, up[...], 1, 0)


def mlp_grads_kernel(hidden, grad, grad_pre, normed, down_out, up_out):
    down_out[...] = dot(hidden[...], grad[...], 0, 0).astype(bf16)
    up_out[...] = dot(grad_pre[...], normed[...], 0, 0).astype(bf16)


def mlp_call(kernel, name, operands, kinds, results, result_kinds, rows, model, hidden):
    chunk = 512
    specs = {
        "rows": whole((rows, model)),
        "wide": pl.BlockSpec((rows, chunk), lambda j: (0, j)),
        "tall": pl.BlockSpec((chunk, model), lambda j: (j, 0)),
        "line": pl.BlockSpec((1, chunk), lambda j: (0, j)),
    }
    shapes = {
        "rows": (rows, model),
        "wide": (rows, hidden),
        "tall": (hidden, model),
        "line": (1, hidden),
    }
    return pl.pallas_call(
        kernel,
        grid=(hidden // chunk,),
        in_specs=[specs[kind] for kind in kinds],
        out_specs=[specs[kind] for kind in result_kinds],
        out_shape=[
            jax.ShapeDtypeStruct(shapes[kind], dtype) for kind, dtype in zip(result_kinds, results)
        ],
        compiler_params=pltpu.CompilerParams(vmem_limit_bytes=56 * MIB),
        cost_estimate=pl.CostEstimate(
            flops=4 * rows * model * hidden, bytes_accessed=8 * rows * hidden, transcendentals=0
        ),
        name=name,
    )(*operands)


def place_kernel(given, out):
    count, width, length = given.shape
    out[...] = jnp.transpose(given[...].reshape(count * width, length)).astype(f32)


def place(gathered, width):
    heads, _, length = gathered.shape
    count = 4
    groups = heads // count
    return pl.pallas_call(
        place_kernel,
        grid=(3, groups),
        in_specs=[pl.BlockSpec((count, width, length), lambda c, i: (i, c, 0))],
        out_specs=pl.BlockSpec((length, count * width), lambda c, i: (0, c * groups + i)),
        out_shape=jax.ShapeDtypeStruct((length, 3 * heads * width), f32),
        compiler_params=pltpu.CompilerParams(vmem_limit_bytes=32 * MIB),
        name="place",
    )(gathered)


def local(
    groups,
    activations,
    block_order,
    qkv_weight,
    qv_bias,
    proj_weight,
    proj_bias,
    up_weight,
    up_bias,
    down_weight,
    down_bias,
    norm_gains,
    norm_biases,
    cotangent,
):
    _, rows, model = activations.shape
    blk = rows // 2
    width = model // HEADS
    ctx = ("r", "h")
    everywhere = ("r", "h", "wt")
    devices = groups * HEADS
    weight_parts = lax.axis_size("wt")
    head = lax.axis_index("h")
    group = lax.axis_index("r")
    part = lax.axis_index("wt")

    small = (qv_bias, proj_bias, up_bias, down_bias, norm_gains, norm_biases)
    packed = jnp.concatenate([array.reshape(-1) for array in small])
    gathered = lax.all_gather(packed, "wt", axis=0)
    pieces, start = [], 0
    for array in small:
        piece = gathered[:, start : start + array.size].reshape((weight_parts,) + array.shape)
        start += array.size
        if array.ndim == 2:
            piece = jnp.transpose(piece, (1, 0, 2)).reshape(array.shape[0], -1)
        else:
            piece = piece.reshape(-1)
        pieces.append(piece.astype(f32))
    qvbias, projbias, upbias, downbias, gains, shifts = pieces

    inputs = activations.reshape(rows, model).astype(f32)
    upstream = cotangent.reshape(rows, model).astype(f32)
    a1 = layer_norm(inputs, gains[0], shifts[0]).astype(bf16)
    a1_full = lax.all_gather(a1, ctx, axis=0, tiled=True)

    mine = lax.dynamic_index_in_dim(
        qkv_weight.reshape(-1, 3, HEADS, width), head, axis=2, keepdims=False
    )
    mine = lax.all_gather(mine.reshape(-1, 3 * width), "wt", axis=0, tiled=True)
    scale = 1.0 / math.sqrt(width)
    mine = jnp.concatenate(
        [mine[:, :width] * bf16(scale), mine[:, 2 * width :], mine[:, width : 2 * width]], axis=1
    )
    q_bias = lax.dynamic_slice(qvbias, (head * width,), (width,))
    v_bias = lax.dynamic_slice(qvbias, (model + head * width,), (width,))
    bias = jnp.concatenate([q_bias * scale, v_bias, jnp.zeros_like(q_bias)])

    lows = block_order.reshape(devices, 2)[:, 0]
    numbers = jnp.arange(devices, dtype=jnp.int32)
    owner = jnp.sum(jnp.where(lows[None, :] == numbers[:, None], numbers[None, :], 0), axis=1)
    owner = jnp.concatenate([owner, owner[::-1]]).astype(jnp.int32)
    is_high = (jnp.arange(2 * devices, dtype=jnp.int32) >= devices).astype(jnp.int32)
    slot_of = 2 * owner + is_high

    half = devices * blk
    q_t, k_n, v_t = project(slot_of, a1_full, mine, bias[None, :], blk, width)
    out_low, log_low, slots_low = forward(False, owner, q_t, k_n, v_t, blk)
    out_high, log_high, slots_high = forward(True, owner, q_t, k_n, v_t, blk)

    def to_tokens(array):
        own = lax.dynamic_slice_in_dim(array, group * HEADS, HEADS, 0)
        return lax.all_to_all(own, "h", 0, 0, tiled=True).reshape(-1, blk)

    def to_heads(array):
        array = lax.all_to_all(array.reshape(HEADS, width, blk), "h", 0, 0, tiled=True)
        if groups > 1:
            array = lax.all_gather(array, "r", axis=0, tiled=True)
        return array

    attended_t = jnp.concatenate([to_tokens(slots_low), to_tokens(slots_high)], axis=1)

    full_proj = lax.all_gather(proj_weight, "wt", axis=0, tiled=True)
    up_full = lax.all_gather(up_weight, "wt", axis=0, tiled=True)
    down_full = lax.all_gather(down_weight, "wt", axis=0, tiled=True)
    full_qkv = lax.all_gather(qkv_weight, "wt", axis=0, tiled=True)

    proj_pre = dot(attended_t, full_proj, 0, 0) + projbias
    residual = inputs + layer_norm(proj_pre, gains[1], shifts[1])
    normed_mid = layer_norm(residual, gains[2], shifts[2]).astype(bf16)
    sizes = (rows, model, up_full.shape[0])
    hidden, slope, branch = mlp_call(
        mlp_forward_kernel,
        "mlp_forward",
        (normed_mid, up_full, upbias[None, :], down_full),
        ("rows", "tall", "line", "tall"),
        (bf16, bf16, f32),
        ("wide", "wide", "rows"),
        *sizes,
    )
    branch = branch + downbias
    layer_output = (residual + layer_norm(branch, gains[3], shifts[3])).astype(bf16)

    grad_branch, gain_three, shift_three = norm_backward(branch, gains[3], shifts[3], upstream)
    grad_branch = grad_branch.astype(bf16)
    grad_pre, up_sums, grad_mid = mlp_call(
        mlp_backward_kernel,
        "mlp_backward",
        (grad_branch, down_full, slope, up_full),
        ("rows", "tall", "wide", "tall"),
        (bf16, f32, f32),
        ("wide", "line", "rows"),
        *sizes,
    )
    grad_residual, gain_two, shift_two = norm_backward(residual, gains[2], shifts[2], grad_mid)
    grad_residual = upstream + grad_residual
    grad_proj_pre, gain_one, shift_one = norm_backward(
        proj_pre, gains[1], shifts[1], grad_residual
    )
    grad_proj_pre = grad_proj_pre.astype(bf16)
    grad_attended_t = dot(full_proj, grad_proj_pre, 1, 1).astype(bf16)
    given_high = to_heads(grad_attended_t[:, blk:])
    given_low = to_heads(grad_attended_t[:, :blk])

    grad_downward, grad_upward = mlp_call(
        mlp_grads_kernel,
        "mlp_grads",
        (hidden, grad_branch, grad_pre, normed_mid),
        ("wide", "rows", "wide", "rows"),
        (bf16, bf16),
        ("tall", "tall"),
        *sizes,
    )
    grad_proj = dot(attended_t, grad_proj_pre, 1, 0).astype(bf16)

    def own_rows(array):
        length = array.shape[0] // weight_parts
        return lax.dynamic_slice_in_dim(array, part * length, length, 0)

    early = jnp.concatenate(
        [
            up_sums[0],
            jnp.sum(grad_branch.astype(f32), axis=0),
            jnp.sum(grad_proj_pre.astype(f32), axis=0),
            gain_one,
            gain_two,
            gain_three,
            shift_one,
            shift_two,
            shift_three,
        ]
    ).astype(bf16)
    grad_proj = jnp.concatenate([grad_proj, early.reshape(-1, model)], axis=0)
    given_high, grad_downward, grad_upward, grad_proj = lax.optimization_barrier(
        (given_high, grad_downward, grad_upward, grad_proj)
    )
    summed = lax.psum((grad_downward, grad_upward, grad_proj), everywhere)
    grad_downward, grad_upward, grad_proj = summed
    early = grad_proj[model:].astype(f32).reshape(-1)
    grad_proj = grad_proj[:model]
    grad_proj = own_rows(grad_proj).astype(f32)
    hidden_width = up_full.shape[0]
    grad_upbias = own_rows(early[:hidden_width])
    early = early[hidden_width:].reshape(8, model)
    grad_downbias = own_rows(early[0])
    grad_projbias = own_rows(early[1])

    def token_grads(array):
        own = lax.dynamic_slice_in_dim(array, group * HEADS, HEADS, 0)
        own = lax.all_to_all(own, "h", 0, 0, tiled=True)
        own = own.reshape(HEADS, -1, width, array.shape[2])
        return jnp.transpose(own, (1, 0, 2, 3)).reshape(-1, array.shape[2])

    grad_t, grad_n, delta, q_n = delta_rows(True, owner, given_high, out_high, q_t)
    high = (q_t[:, half:], q_n, grad_t, grad_n, log_high, delta)
    query_sum, high_pair = backward("high", owner, high, k_n, v_t, (), (), blk)
    high_tokens = token_grads(high_pair)
    grad_t, grad_n, delta, q_n = delta_rows(False, owner, given_low, out_low, q_t)
    low = (q_t[:, :half], q_n, grad_t, grad_n, log_low, delta)
    key_sum, value_sum, low_query = backward("low", owner, low, k_n, v_t, (), (), blk)
    starts = (query_sum, key_sum, value_sum, low_query)
    query_sum, first = backward("first", owner, high, k_n, v_t, starts, (high_tokens,), blk)
    first_tokens = token_grads(first)
    starts = (query_sum, key_sum, value_sum)
    query, second = backward("second", owner, high, k_n, v_t, starts, (), blk)
    query, first_tokens = lax.optimization_barrier((query, first_tokens))
    query_tokens = token_grads(query)

    def own_columns(array):
        length = array.shape[1] // weight_parts
        return lax.dynamic_slice_in_dim(array, part * length, length, 1)

    columns_grad, grad_downward, grad_upward = weight_grad(
        part.astype(jnp.int32),
        high_pair,
        first,
        query,
        second,
        a1_full,
        grad_downward,
        grad_upward,
        weight_parts,
        (first_tokens,),
    )
    columns_grad, query_tokens = lax.optimization_barrier((columns_grad, query_tokens))
    columns_grad = lax.all_to_all(columns_grad, "wt", 0, 0, tiled=True)
    columns_grad = jnp.sum(columns_grad.astype(f32), axis=0).astype(bf16)
    columns_grad, second = lax.optimization_barrier((columns_grad, second))
    second_tokens = token_grads(second)
    all_columns = lax.all_gather(columns_grad, "h", axis=0)
    grad_qkv = place(all_columns, width)
    sums = all_columns[:, 3 * width : 3 * width + 3, :width].astype(f32)
    sums = jnp.transpose(sums, (1, 0, 2)).reshape(3, model)
    grad_qvbias = own_rows(jnp.concatenate([sums[0], sums[2]]))

    own_weight = qkv_weight.astype(f32)
    shift_zero = jnp.sum(own_weight * sums.reshape(1, -1), axis=1)
    gain_zero = jnp.sum(own_weight * grad_qkv, axis=1)
    first_norm = own_columns(jnp.stack([gains[0], shifts[0]]))
    gain_zero = (gain_zero - first_norm[1] * shift_zero) / first_norm[0]

    piece = blk // 2
    low_key = [first_tokens[model:, :piece], second_tokens[:model]]
    low_value = [first_tokens[model:, piece:], second_tokens[model:]]
    low_rows = [
        first_tokens[:model],
        jnp.concatenate(low_key, axis=1),
        jnp.concatenate(low_value, axis=1),
    ]
    high_rows = [query_tokens, high_tokens]
    grads_t = jnp.concatenate(
        [jnp.concatenate(low_rows, axis=0), jnp.concatenate(high_rows, axis=0)], axis=1
    )
    grad_normed = dot(grads_t, full_qkv, 0, 1)
    grad_inputs, _, _ = norm_backward(inputs, gains[0], shifts[0], grad_normed)
    input_grad = (grad_residual + grad_inputs).reshape(1, rows, model)
    early = own_columns(early)
    grad_gains = jnp.concatenate([gain_zero[None], early[2:5]], axis=0)
    grad_biases = jnp.concatenate([shift_zero[None], early[5:8]], axis=0)
    return (
        layer_output.reshape(1, rows, model),
        input_grad,
        grad_qkv,
        grad_qvbias,
        grad_proj,
        grad_projbias,
        grad_upward,
        grad_upbias,
        grad_downward,
        grad_downbias,
        grad_gains,
        grad_biases,
    )


def solution(mesh):
    groups = mesh.shape["ctx"] // HEADS
    split = Mesh(
        mesh.devices.reshape(groups, HEADS, mesh.shape["wt"]), ("r", "h", "wt")
    )
    tokens = P("wt", ("r", "h"), None)
    rows, flat, cols = P("wt", None), P("wt"), P(None, "wt")
    return jax.shard_map(
        functools.partial(local, groups),
        mesh=split,
        in_specs=(tokens, P(), rows, flat, rows, flat, rows, flat, rows, flat, cols, cols, tokens),
        out_specs=(tokens, tokens, rows, flat, rows, flat, rows, flat, rows, flat, cols, cols),
        check_vma=False,
    )
```

```python
import functools
import math

import jax
import jax.numpy as jnp
from jax import lax
from jax.experimental import pallas as pl
from jax.experimental.pallas import tpu as pltpu
from jax.sharding import Mesh
from jax.sharding import PartitionSpec as P

HEADS = 16
ALPHA = 32.0
EPS = 1e-05
NEG = -1e30
bf16 = jnp.bfloat16
f32 = jnp.float32
MIB = 1 << 20


def layer_norm(values, norm_gain, norm_shift):
    average = jnp.mean(values, axis=-1, keepdims=True)
    centered = values - average
    variance = jnp.mean(centered * centered, axis=-1, keepdims=True)
    return centered * lax.rsqrt(variance + EPS) * norm_gain + norm_shift


def gelu_and_slope(values):
    squared = values * values
    scale = math.sqrt(2.0 / math.pi)
    bent = jnp.tanh(scale * (values * (1.0 + 0.044715 * squared)))
    half = 0.5 * (1.0 + bent)
    slope = half + (0.5 * scale) * values * (1.0 - bent * bent) * (1.0 + 0.134145 * squared)
    return values * half, slope


def dot(a, b, ca, cb):
    return lax.dot_general(a, b, (((ca,), (cb,)), ((), ())), preferred_element_type=f32)


def columns(index, width):
    return pl.ds(pl.multiple_of(index * width, width), width)


def whole(shape):
    return pl.BlockSpec(shape, lambda *_: (0,) * len(shape), pipeline_mode=pl.Buffered(1))


def project_kernel(table, *refs):
    blocks, (weight, bias, q_t, k_n, v_t) = refs[:-5], refs[-5:]
    width = k_n.shape[1]
    for number, rows in enumerate(blocks):
        blk = rows.shape[0]
        part = slice(number * blk, (number + 1) * blk)
        heads = (dot(rows[...], weight[...], 1, 0) + bias[...]).astype(bf16)
        turned = jnp.transpose(heads[:, : 2 * width])
        q_t[:, part] = turned[:width]
        v_t[:, part] = turned[width:]
        k_n[part, :] = heads[:, 2 * width :]


def project(table, a1_full, weight, bias, blk, width):
    tokens, model = a1_full.shape
    count = 4
    tile = count * blk
    turned = pl.BlockSpec((width, tile), lambda i, t: (0, i))
    straight = pl.BlockSpec((tile, width), lambda i, t: (i, 0))

    def block(number):
        return pl.BlockSpec((blk, model), lambda i, t: (t[count * i + number], 0))

    return pl.pallas_call(
        project_kernel,
        grid_spec=pltpu.PrefetchScalarGridSpec(
            num_scalar_prefetch=1,
            grid=(tokens // tile,),
            in_specs=[block(number) for number in range(count)]
            + [whole(weight.shape), whole(bias.shape)],
            out_specs=[turned, straight, turned],
        ),
        out_shape=[
            jax.ShapeDtypeStruct((width, tokens), bf16),
            jax.ShapeDtypeStruct((tokens, width), bf16),
            jax.ShapeDtypeStruct((width, tokens), bf16),
        ],
        compiler_params=pltpu.CompilerParams(vmem_limit_bytes=48 * MIB),
        cost_estimate=pl.CostEstimate(
            flops=8 * tokens * model * width, bytes_accessed=2 * tokens * model, transcendentals=0
        ),
        name="project",
    )(table, *([a1_full] * count), weight, bias)


def forward_kernel(base, table, q_t, k_n, v_t, out_t, log_total, out_slots, scores):
    _, width, blk = out_slots.shape
    tile = q_t.shape[1]
    step = base + pl.program_id(0)
    query = q_t[...]

    def score(index):
        return dot(k_n[columns(index, blk), :], query, 1, 0)

    def prepare(index, slot):
        tile_scores = score(index)
        scores[slot] = tile_scores
        return jnp.max(tile_scores, axis=0, keepdims=True)

    ones = jnp.ones((16, blk), bf16)

    def absorb(index, tile_scores, peak, summed, tile_peak):
        new_peak = jnp.maximum(peak, tile_peak)
        weights = jnp.exp(tile_scores - new_peak).astype(bf16)
        keep = jnp.exp(peak - new_peak)
        values = jnp.concatenate([v_t[:, columns(index, blk)], ones], axis=0)
        return new_peak, summed * keep + dot(values, weights, 1, 0)

    def body(pair, carry):
        peak, summed, tile_peak = carry
        for slot in range(2):
            next_peak = prepare(2 * pair + slot + 1, 1 - slot)
            peak, summed = absorb(2 * pair + slot, scores[slot], peak, summed, tile_peak)
            tile_peak = next_peak
        return peak, summed, tile_peak

    carry = (
        jnp.full((1, tile), -jnp.inf, f32),
        jnp.zeros((width + 16, tile), f32),
        prepare(0, 0),
    )
    peak, summed, _ = lax.fori_loop(0, step, body, carry)
    for half in range(2):
        part = query[:, half * blk :]
        shape = (blk, tile - half * blk)
        key_pos = lax.broadcasted_iota(jnp.int32, shape, 0)
        query_pos = lax.broadcasted_iota(jnp.int32, shape, 1)
        tile_scores = dot(k_n[columns(2 * step + half, blk), :], part, 1, 0)
        tile_scores = jnp.where(query_pos >= key_pos, tile_scores, NEG)
        tile_peak = jnp.max(tile_scores, axis=0, keepdims=True)
        state = absorb(2 * step + half, tile_scores, peak, summed, tile_peak)
        if half == 0:
            left = tuple(array[:, :blk] for array in state)
            peak, summed = (array[:, blk:] for array in state)
    peak, summed = (
        jnp.concatenate([first, second], axis=1) for first, second in zip(left, state)
    )
    total = summed[width : width + 1]
    result = summed[:width] / total
    out_t[...] = result
    log_total[...] = peak + jnp.log(total)
    low = result.astype(bf16)
    for half in range(2):
        out_slots[table[2 * step + half]] = low[:, half * blk : (half + 1) * blk]


def forward(high, table, q_t, k_n, v_t, blk):
    width, tokens = q_t.shape
    slots = tokens // (2 * blk)
    tile = 2 * blk
    steps = slots // 2
    base = steps if high else 0
    seen = tokens if high else tokens // 2
    return pl.pallas_call(
        functools.partial(forward_kernel, base),
        grid_spec=pltpu.PrefetchScalarGridSpec(
            num_scalar_prefetch=1,
            grid=(steps,),
            in_specs=[
                pl.BlockSpec((width, tile), lambda i, t: (0, base + i)),
                whole((seen, width)),
                whole((width, seen)),
            ],
            out_specs=[
                pl.BlockSpec((width, tile), lambda i, t: (0, i)),
                pl.BlockSpec((1, tile), lambda i, t: (0, i)),
                whole((slots, width, blk)),
            ],
            scratch_shapes=[pltpu.VMEM((2, blk, tile), f32)],
        ),
        out_shape=[
            jax.ShapeDtypeStruct((width, tokens // 2), f32),
            jax.ShapeDtypeStruct((1, tokens // 2), f32),
            jax.ShapeDtypeStruct((slots, width, blk), bf16),
        ],
        compiler_params=pltpu.CompilerParams(vmem_limit_bytes=56 * MIB),
        cost_estimate=pl.CostEstimate(
            flops=(6 if high else 2) * tokens * tokens * width,
            bytes_accessed=12 * tokens * width,
            transcendentals=(3 if high else 1) * tokens * tokens // 8,
        ),
        name="forward_high" if high else "forward_low",
    )(table, q_t, k_n, v_t)


def delta_kernel(table, given, out_t, q_t, grad_t, grad_n, delta, q_n):
    block = given[0]
    grad_t[...] = block
    wide = block.astype(f32)
    delta[...] = jnp.sum(wide * out_t[...], axis=0, keepdims=True)
    grad_n[...] = jnp.transpose(wide).astype(bf16)
    q_n[...] = jnp.transpose(q_t[...].astype(f32)).astype(bf16)


def delta_rows(high, table, given, out_t, q_t):
    slots, width, blk = given.shape
    half = slots * blk
    base = slots if high else 0
    return pl.pallas_call(
        delta_kernel,
        grid_spec=pltpu.PrefetchScalarGridSpec(
            num_scalar_prefetch=1,
            grid=(slots,),
            in_specs=[
                pl.BlockSpec((1, width, blk), lambda p, t: (t[base + p], 0, 0)),
                pl.BlockSpec((width, blk), lambda p, t: (0, p)),
                pl.BlockSpec((width, blk), lambda p, t: (0, base + p)),
            ],
            out_specs=[
                pl.BlockSpec((width, blk), lambda p, t: (0, p)),
                pl.BlockSpec((blk, width), lambda p, t: (p, 0)),
                pl.BlockSpec((1, blk), lambda p, t: (0, p)),
                pl.BlockSpec((blk, width), lambda p, t: (p, 0)),
            ],
        ),
        out_shape=[
            jax.ShapeDtypeStruct((width, half), bf16),
            jax.ShapeDtypeStruct((half, width), bf16),
            jax.ShapeDtypeStruct((1, half), f32),
            jax.ShapeDtypeStruct((half, width), bf16),
        ],
        compiler_params=pltpu.CompilerParams(vmem_limit_bytes=32 * MIB),
        name="delta_high" if high else "delta_low",
    )(table, given, out_t, q_t)


def backward_kernel(kind, base, after, *refs):
    table, q_t, q_n, grad_t, grad_n, log_total, delta, k_n, v_t = refs[:9]
    refs = refs[9:]
    cross = kind in ("first", "second")
    query_out = key_out = value_out = None
    if cross:
        (query_start, key_start, value_start), refs = refs[:3], refs[3:]
    if kind == "first":
        low_query, refs = refs[0], refs[1:]
    refs = refs[after:]
    if kind == "second":
        query_slots, refs = refs[0], refs[1:]
    if kind in ("high", "first"):
        query_out, refs = refs[0], refs[1:]
    elif kind == "low":
        (key_out, value_out), refs = refs[:2], refs[2:]
    out_slots, refs = refs[0], refs[1:]
    scores, grads, query_sum, key_sum, value_sum = refs
    _, tile, blk = scores.shape
    slots = out_slots.shape[0]
    width = q_t.shape[0]
    piece = blk // 2
    step = pl.program_id(0)

    @pl.when(step == 0)
    def _():
        if cross:
            query_sum[...] = query_start[...]
        else:
            query_sum[...] = jnp.zeros_like(query_sum)
        if kind == "first":
            out_slots[:, :width] = low_query[...]

    keys = k_n[...].reshape(tile, width)
    keys_t = jnp.transpose(keys.astype(f32)).astype(bf16)
    if cross:
        start = piece if kind == "second" else 0
        starts = range(start, v_t.shape[1], blk)
        values = jnp.concatenate([v_t[:, at : at + piece] for at in starts], axis=1)
    else:
        values = v_t[...]
    values = jnp.transpose(values.astype(f32)).astype(bf16)
    if cross:
        key_sum[...] = key_start[...].reshape(tile, width)
        value_sum[...] = value_start[...].reshape(tile, width)
    else:
        key_sum[...] = jnp.zeros_like(key_sum)
        value_sum[...] = jnp.zeros_like(value_sum)

    def prepare(index, slot):
        at = columns(index, blk)
        scores[slot] = dot(keys, q_t[:, at], 1, 0)
        grads[slot] = dot(values, grad_t[:, at], 1, 0)

    def absorb(index, tile_scores, prob_grads):
        at = columns(index, blk)
        rows = tile_scores.shape[0]
        probs = jnp.exp(tile_scores - log_total[:, at])
        score_grads = (probs * (prob_grads - delta[:, at])).astype(bf16)
        value_sum[:rows] += dot(probs.astype(bf16), grad_n[at, :], 1, 0)
        key_sum[:rows] += dot(score_grads, q_n[at, :], 1, 0)
        query_sum[:, at] += dot(keys_t[:, :rows], score_grads, 1, 0)

    def diagonal(half):
        index = 2 * step + half
        at = columns(index, blk)
        shape = ((half + 1) * blk, blk)
        key_pos = lax.broadcasted_iota(jnp.int32, shape, 0)
        query_pos = half * blk + lax.broadcasted_iota(jnp.int32, shape, 1)
        tile_scores = dot(keys[: shape[0]], q_t[:, at], 1, 0)
        tile_scores = jnp.where(query_pos >= key_pos, tile_scores, NEG)
        absorb(index, tile_scores, dot(values[: shape[0]], grad_t[:, at], 1, 0))

    def sweep(first, pairs):
        prepare(first, 0)

        def body(pair, carry):
            index = first + 2 * pair
            prepare(index + 1, 1)
            absorb(index, scores[0], grads[0])
            prepare(jnp.minimum(index + 2, slots - 1), 0)
            absorb(index + 1, scores[1], grads[1])
            return carry

        lax.fori_loop(0, pairs, body, 0)

    if cross:
        sweep(0, slots // 2)
    else:
        for half in range(2):
            diagonal(half)

        @pl.when(2 * step + 2 < slots)
        def _():
            sweep(2 * step + 2, slots // 2 - 1 - step)

    def query_grads(index):
        return (query_sum[:, columns(index, blk)] * 0.125).astype(bf16)

    if kind == "low":
        key_out[...] = key_sum[...]
        value_out[...] = value_sum[...]
        for half in range(2):
            index = 2 * step + half
            out_slots[table[base + index]] = query_grads(index)
    else:
        key_t = jnp.transpose(key_sum[...]).astype(bf16)
        value_t = jnp.transpose(value_sum[...]).astype(bf16)
        wide = blk if kind == "high" else piece
        for number in range(tile // wide):
            slot = table[base + tile // wide * step + number]
            part = slice(number * wide, (number + 1) * wide)
            if kind == "first":
                out_slots[slot, width:, :piece] = key_t[:, part]
                out_slots[slot, width:, piece:] = value_t[:, part]
            else:
                out_slots[slot, :width] = key_t[:, part]
                out_slots[slot, width:] = value_t[:, part]

    @pl.when(step == pl.num_programs(0) - 1)
    def _():
        if query_out is not None:
            query_out[...] = query_sum[...]
        if kind == "second":

            def finish(index, carry):
                query_slots[table[slots + index]] = query_grads(index)
                return carry

            lax.fori_loop(0, slots, finish, 0)


def backward(kind, table, queries, k_n, v_t, starts, after, blk):
    width, half = queries[0].shape
    slots = half // blk
    tile = 2 * blk
    piece = blk // 2
    cross = kind in ("first", "second")
    second = 1 if kind == "second" else 0
    steps = slots // 4 if cross else slots // 2
    skip = slots // 2 if kind == "high" else 0
    if cross:
        straight = pl.BlockSpec((4, 1, piece, width), lambda i, t: (i, second, 0, 0))
        k_n = k_n.reshape(-1, 2, piece, width)
        starts = (
            (starts[0],)
            + tuple(array.reshape(-1, 2, piece, width) for array in starts[1:3])
            + tuple(starts[3:])
        )
    else:
        straight = pl.BlockSpec((tile, width), lambda i, t: (skip + i, 0))
    in_specs = [whole(array.shape) for array in queries] + [
        straight,
        pl.BlockSpec((width, 4 * blk if cross else tile), lambda i, t: (0, skip + i)),
    ]
    if cross:
        in_specs += [whole((width, half)), straight, straight]
        in_specs += [whole(array.shape) for array in starts[3:]]
    in_specs += [pl.BlockSpec(memory_space=pl.ANY)] * len(after)
    rows = width if kind == "low" else 2 * width
    held = (slots, rows, piece if kind == "second" else blk)
    out_specs = [whole(held)]
    out_shape = [jax.ShapeDtypeStruct(held, bf16)]
    if kind in ("high", "first"):
        out_specs = [whole((width, half))] + out_specs
        out_shape = [jax.ShapeDtypeStruct((width, half), f32)] + out_shape
    elif kind == "second":
        out_specs = [whole((slots, width, blk))] + out_specs
        out_shape = [jax.ShapeDtypeStruct((slots, width, blk), bf16)] + out_shape
    elif kind == "low":
        out_specs = [straight, straight] + out_specs
        out_shape = [jax.ShapeDtypeStruct((half, width), f32)] * 2 + out_shape
    return pl.pallas_call(
        functools.partial(backward_kernel, kind, 2 * skip, len(after)),
        grid_spec=pltpu.PrefetchScalarGridSpec(
            num_scalar_prefetch=1,
            grid=(steps,),
            in_specs=in_specs,
            out_specs=out_specs,
            scratch_shapes=[
                pltpu.VMEM((2, tile, blk), f32),
                pltpu.VMEM((2, tile, blk), f32),
                pltpu.VMEM((width, half), f32),
                pltpu.VMEM((tile, width), f32),
                pltpu.VMEM((tile, width), f32),
            ],
        ),
        out_shape=out_shape,
        compiler_params=pltpu.CompilerParams(vmem_limit_bytes=56 * MIB),
        cost_estimate=pl.CostEstimate(
            flops=4 * half * half * width,
            bytes_accessed=32 * half * width,
            transcendentals=half * half // 8,
        ),
        name="backward_" + kind,
    )(table, *queries, k_n, v_t, *starts, *after)


def weight_kernel(part, high_pair, first, query, second, a1, down, up, *refs):
    out, down_out, up_out, total, sums = refs[-5:]
    _, width, blk = query.shape
    down_out[...] = down[...].astype(f32)
    up_out[...] = up[...].astype(f32)
    piece = blk // 2
    parts, rows, length = out.shape
    step = pl.program_id(0)

    @pl.when(step == 0)
    def _():
        total[...] = jnp.zeros_like(total)
        sums[...] = jnp.zeros_like(sums)

    low_key = jnp.concatenate([first[0, width:, :piece], second[0, :width]], axis=1)
    low_value = jnp.concatenate([first[0, width:, piece:], second[0, width:]], axis=1)
    low = jnp.concatenate([first[0, :width], low_key, low_value], axis=0)
    high = jnp.concatenate([query[0], high_pair[0]], axis=0)
    total[...] += dot(low, a1[:blk], 1, 0) + dot(high, a1[blk:], 1, 0)
    wide = low.astype(f32) + high.astype(f32)
    for at in range(0, blk, 128):
        sums[...] += wide[:, at : at + 128]

    @pl.when(step == pl.num_programs(0) - 1)
    def _():
        row = jnp.sum(jnp.transpose(sums[...]), axis=0, keepdims=True)
        tail = [row[:, number * width : (number + 1) * width] for number in range(3)]
        tail = jnp.concatenate(tail, axis=0)
        tail = jnp.concatenate([tail, jnp.zeros((3, length - width), f32)], axis=1)
        tail = jnp.concatenate([tail, jnp.zeros((rows - 3 * width - 3, length), f32)], axis=0)
        for number in range(parts):
            own = total[:, number * length : (number + 1) * length]
            out[number] = jnp.concatenate([own, tail], axis=0).astype(bf16)


def weight_grad(part, high_pair, first, query, second, a1_full, down, up, parts, after):
    slots, width, blk = query.shape
    tokens, model = a1_full.shape
    rows = 3 * width
    shape = (parts, rows + 16, model // parts)
    given = (high_pair, first, query, second)
    own = down.shape[0] // parts
    strip = own // slots
    summed = pl.BlockSpec((strip, model), lambda s, t: (t[0] * slots + s, 0))
    kept = pl.BlockSpec((strip, model), lambda s, t: (s, 0))
    return pl.pallas_call(
        weight_kernel,
        grid_spec=pltpu.PrefetchScalarGridSpec(
            num_scalar_prefetch=1,
            grid=(slots,),
            in_specs=[
                pl.BlockSpec((1,) + array.shape[1:], lambda s, t: (s, 0, 0)) for array in given
            ]
            + [pl.BlockSpec((2 * blk, model), lambda s, t: (s, 0)), summed, summed]
            + [pl.BlockSpec(memory_space=pl.ANY)] * len(after),
            out_specs=[whole(shape), kept, kept],
            scratch_shapes=[pltpu.VMEM((rows, model), f32), pltpu.VMEM((rows, 128), f32)],
        ),
        out_shape=[jax.ShapeDtypeStruct(shape, bf16)]
        + [jax.ShapeDtypeStruct((own, model), f32)] * 2,
        compiler_params=pltpu.CompilerParams(vmem_limit_bytes=48 * MIB),
        cost_estimate=pl.CostEstimate(
            flops=2 * rows * tokens * model, bytes_accessed=2 * tokens * model, transcendentals=0
        ),
        name="weight_grad",
    )(part.reshape(1), *given, a1_full, down, up, *after)


def normalize(values):
    centered = values - jnp.mean(values, axis=-1, keepdims=True)
    factor = lax.rsqrt(jnp.mean(centered * centered, axis=-1, keepdims=True) + EPS)
    return centered * factor, factor


def normalize_backward(normal, factor, gain, upstream):
    scaled = upstream * gain
    along = jnp.mean(scaled * normal, axis=-1, keepdims=True)
    return factor * (scaled - jnp.mean(scaled, axis=-1, keepdims=True) - normal * along)


def over_rows(rows, body, count, width):
    strip = 128

    def one(index, sums):
        return body(pl.ds(pl.multiple_of(index * strip, strip), strip), sums)

    zero = tuple(jnp.zeros((1, width), f32) for _ in range(count))
    return lax.fori_loop(0, rows // strip, one, zero)


def column_sum(values):
    return jnp.sum(values, axis=0, keepdims=True)


def mlp_forward_kernel(
    normed, up, up_bias, down, down_bias, residual, upstream, gain, shift,
    hidden, slope, layer_output, grad_branch, sums, total,
):
    step = pl.program_id(0)

    @pl.when(step == 0)
    def _():
        total[...] = jnp.zeros_like(total)

    value, bend = gelu_and_slope(dot(normed[...], up[...], 1, 1) + up_bias[...])
    low = value.astype(bf16)
    hidden[...] = low
    slope[...] = bend.astype(bf16)
    total[...] += dot(low, down[...], 1, 0)

    @pl.when(step == pl.num_programs(0) - 1)
    def _():
        def strip(at, carry):
            normal, factor = normalize(total[at, :] + down_bias[...])
            output = residual[at, :] + normal * gain[...] + shift[...]
            layer_output[at, :] = output.astype(bf16)
            given = upstream[at, :].astype(f32)
            grad = normalize_backward(normal, factor, gain[...], given).astype(bf16)
            grad_branch[at, :] = grad
            new = (given * normal, given, grad.astype(f32))
            return tuple(old + column_sum(part) for old, part in zip(carry, new))

        result = over_rows(*[total.shape[0], strip, 3, total.shape[1]])
        for number in range(3):
            sums[number : number + 1] = result[number]


def mlp_backward_kernel(
    grad, down, slope, up, residual, proj_pre, upstream, gain_one, gain_two,
    grad_pre, up_sums, grad_residual, grad_proj_pre, sums, total,
):
    step = pl.program_id(0)

    @pl.when(step == 0)
    def _():
        total[...] = jnp.zeros_like(total)

    low = (dot(grad[...], down[...], 1, 1) * slope[...].astype(f32)).astype(bf16)
    grad_pre[...] = low
    up_sums[...] = column_sum(low.astype(f32))
    total[...] += dot(low, up[...], 1, 0)

    @pl.when(step == pl.num_programs(0) - 1)
    def _():
        def strip(at, carry):
            grad_mid = total[at, :]
            normal_two, factor = normalize(residual[at, :])
            back = normalize_backward(normal_two, factor, gain_two[...], grad_mid)
            back = upstream[at, :].astype(f32) + back
            grad_residual[at, :] = back
            normal_one, factor = normalize(proj_pre[at, :])
            low = normalize_backward(normal_one, factor, gain_one[...], back).astype(bf16)
            grad_proj_pre[at, :] = low
            new = (back * normal_one, back, grad_mid * normal_two, grad_mid, low.astype(f32))
            return tuple(old + column_sum(part) for old, part in zip(carry, new))

        result = over_rows(*[total.shape[0], strip, 5, total.shape[1]])
        for number in range(5):
            sums[number : number + 1] = result[number]


def mlp_grads_kernel(hidden, grad, grad_pre, normed, down_out, up_out):
    down_out[...] = dot(hidden[...], grad[...], 0, 0).astype(bf16)
    up_out[...] = dot(grad_pre[...], normed[...], 0, 0).astype(bf16)


def mlp_call(kernel, name, operands, kinds, results, result_kinds, rows, model, hidden, kept):
    chunk = 512
    specs = {
        "rows": whole((rows, model)),
        "wide": pl.BlockSpec((rows, chunk), lambda j: (0, j)),
        "tall": pl.BlockSpec((chunk, model), lambda j: (j, 0)),
        "line": pl.BlockSpec((1, chunk), lambda j: (0, j)),
        "row": whole((1, model)),
        "sums": whole((8, model)),
    }
    shapes = {
        "rows": (rows, model),
        "wide": (rows, hidden),
        "tall": (hidden, model),
        "line": (1, hidden),
        "sums": (8, model),
    }
    return pl.pallas_call(
        kernel,
        grid=(hidden // chunk,),
        in_specs=[specs[kind] for kind in kinds],
        out_specs=[specs[kind] for kind in result_kinds],
        out_shape=[
            jax.ShapeDtypeStruct(shapes[kind], dtype) for kind, dtype in zip(result_kinds, results)
        ],
        scratch_shapes=[pltpu.VMEM((rows, model), f32)] if kept else [],
        compiler_params=pltpu.CompilerParams(vmem_limit_bytes=56 * MIB),
        cost_estimate=pl.CostEstimate(
            flops=4 * rows * model * hidden, bytes_accessed=8 * rows * hidden, transcendentals=0
        ),
        name=name,
    )(*operands)


def input_kernel(
    first, second, query, high, weight_q, weight_k, weight_v, inputs, grad_residual, gain,
    out, total,
):
    step = pl.program_id(0)
    heads, _, blk = first.shape
    width = query.shape[1]
    piece = blk // 2
    rows = heads * width

    def part(array, start):
        return array[:, start : start + width].reshape(rows, array.shape[2])

    @pl.when(step == 0)
    def _():
        total[...] = jnp.zeros_like(total)

    weight = jnp.concatenate([weight_q[...], weight_k[...], weight_v[...]], axis=1)
    pair = part(first, width)
    key = jnp.concatenate([pair[:, :piece], part(second, 0)], axis=1)
    value = jnp.concatenate([pair[:, piece:], part(second, width)], axis=1)
    low = jnp.concatenate([part(first, 0), key, value], axis=0)
    top = jnp.concatenate([part(query, 0), part(high, 0), part(high, width)], axis=0)
    total[:, :blk] += dot(weight, low, 1, 0)
    total[:, blk:] += dot(weight, top, 1, 0)

    @pl.when(step == pl.num_programs(0) - 1)
    def _():
        def strip(index, carry):
            at = columns(index, 128)
            grad = jnp.transpose(total[:, at])
            normal, factor = normalize(inputs[at, :].astype(f32))
            back = normalize_backward(normal, factor, gain[...], grad)
            out[at, :] = grad_residual[at, :] + back
            return carry

        lax.fori_loop(0, out.shape[0] // 128, strip, 0)


def input_grads(first, second, query, high, weight, inputs, grad_residual, gain):
    heads, width, blk = query.shape
    rows, model = inputs.shape
    count = 4
    steps = heads // count
    given = (first, second, query, high)

    def columns_of(number):
        return pl.BlockSpec((model, count * width), lambda j: (0, number * steps + j))

    return pl.pallas_call(
        input_kernel,
        grid=(steps,),
        in_specs=[pl.BlockSpec((count,) + array.shape[1:], lambda j: (j, 0, 0)) for array in given]
        + [columns_of(number) for number in range(3)]
        + [whole((rows, model)), whole((rows, model)), whole((1, model))],
        out_specs=whole((rows, model)),
        out_shape=jax.ShapeDtypeStruct((rows, model), f32),
        scratch_shapes=[pltpu.VMEM((model, rows), f32)],
        compiler_params=pltpu.CompilerParams(vmem_limit_bytes=56 * MIB),
        cost_estimate=pl.CostEstimate(
            flops=6 * rows * model * model, bytes_accessed=24 * rows * model, transcendentals=0
        ),
        name="input_grads",
    )(*given, weight, weight, weight, inputs, grad_residual, gain)


def place_kernel(given, out):
    count, width, length = given.shape
    out[...] = jnp.transpose(given[...].reshape(count * width, length)).astype(f32)


def place(gathered, width):
    heads, _, length = gathered.shape
    count = 4
    groups = heads // count
    return pl.pallas_call(
        place_kernel,
        grid=(3, groups),
        in_specs=[pl.BlockSpec((count, width, length), lambda c, i: (i, c, 0))],
        out_specs=pl.BlockSpec((length, count * width), lambda c, i: (0, c * groups + i)),
        out_shape=jax.ShapeDtypeStruct((length, 3 * heads * width), f32),
        compiler_params=pltpu.CompilerParams(vmem_limit_bytes=32 * MIB),
        name="place",
    )(gathered)


def local(
    groups,
    activations,
    block_order,
    qkv_weight,
    qv_bias,
    proj_weight,
    proj_bias,
    up_weight,
    up_bias,
    down_weight,
    down_bias,
    norm_gains,
    norm_biases,
    cotangent,
):
    _, rows, model = activations.shape
    blk = rows // 2
    width = model // HEADS
    ctx = ("r", "h")
    everywhere = ("r", "h", "wt")
    devices = groups * HEADS
    weight_parts = lax.axis_size("wt")
    head = lax.axis_index("h")
    group = lax.axis_index("r")
    part = lax.axis_index("wt")

    small = (qv_bias, proj_bias, up_bias, down_bias, norm_gains, norm_biases)
    packed = jnp.concatenate([array.reshape(-1) for array in small])
    gathered = lax.all_gather(packed, "wt", axis=0)
    pieces, start = [], 0
    for array in small:
        piece = gathered[:, start : start + array.size].reshape((weight_parts,) + array.shape)
        start += array.size
        if array.ndim == 2:
            piece = jnp.transpose(piece, (1, 0, 2)).reshape(array.shape[0], -1)
        else:
            piece = piece.reshape(-1)
        pieces.append(piece.astype(f32))
    qvbias, projbias, upbias, downbias, gains, shifts = pieces

    inputs = activations.reshape(rows, model).astype(f32)
    a1 = layer_norm(inputs, gains[0], shifts[0]).astype(bf16)
    a1_full = lax.all_gather(a1, ctx, axis=0, tiled=True)

    mine = lax.dynamic_index_in_dim(
        qkv_weight.reshape(-1, 3, HEADS, width), head, axis=2, keepdims=False
    )
    mine = lax.all_gather(mine.reshape(-1, 3 * width), "wt", axis=0, tiled=True)
    scale = 1.0 / math.sqrt(width)
    mine = jnp.concatenate(
        [mine[:, :width] * bf16(scale), mine[:, 2 * width :], mine[:, width : 2 * width]], axis=1
    )
    q_bias = lax.dynamic_slice(qvbias, (head * width,), (width,))
    v_bias = lax.dynamic_slice(qvbias, (model + head * width,), (width,))
    bias = jnp.concatenate([q_bias * scale, v_bias, jnp.zeros_like(q_bias)])

    lows = block_order.reshape(devices, 2)[:, 0]
    numbers = jnp.arange(devices, dtype=jnp.int32)
    owner = jnp.sum(jnp.where(lows[None, :] == numbers[:, None], numbers[None, :], 0), axis=1)
    owner = jnp.concatenate([owner, owner[::-1]]).astype(jnp.int32)
    is_high = (jnp.arange(2 * devices, dtype=jnp.int32) >= devices).astype(jnp.int32)
    slot_of = 2 * owner + is_high

    half = devices * blk
    q_t, k_n, v_t = project(slot_of, a1_full, mine, bias[None, :], blk, width)
    out_low, log_low, slots_low = forward(False, owner, q_t, k_n, v_t, blk)
    out_high, log_high, slots_high = forward(True, owner, q_t, k_n, v_t, blk)

    def to_tokens(array):
        own = lax.dynamic_slice_in_dim(array, group * HEADS, HEADS, 0)
        return lax.all_to_all(own, "h", 0, 0, tiled=True).reshape(-1, blk)

    def to_heads(array):
        array = lax.all_to_all(array.reshape(HEADS, width, blk), "h", 0, 0, tiled=True)
        if groups > 1:
            array = lax.all_gather(array, "r", axis=0, tiled=True)
        return array

    attended_t = jnp.concatenate([to_tokens(slots_low), to_tokens(slots_high)], axis=1)

    full_proj = lax.all_gather(proj_weight, "wt", axis=0, tiled=True)
    up_full = lax.all_gather(up_weight, "wt", axis=0, tiled=True)
    down_full = lax.all_gather(down_weight, "wt", axis=0, tiled=True)
    full_qkv = lax.all_gather(qkv_weight, "wt", axis=0, tiled=True)

    proj_pre = dot(attended_t, full_proj, 0, 0) + projbias
    residual = inputs + layer_norm(proj_pre, gains[1], shifts[1])
    normed_mid = layer_norm(residual, gains[2], shifts[2]).astype(bf16)
    sizes = (rows, model, up_full.shape[0])
    given = cotangent.reshape(rows, model)
    hidden, slope, layer_output, grad_branch, sums_three = mlp_call(
        mlp_forward_kernel,
        "mlp_forward",
        (normed_mid, up_full, upbias[None, :], down_full, downbias[None, :], residual, given)
        + (gains[3:4], shifts[3:4]),
        ("rows", "tall", "line", "tall", "row", "rows", "rows", "row", "row"),
        (bf16, bf16, bf16, bf16, f32),
        ("wide", "wide", "rows", "rows", "sums"),
        *sizes,
        True,
    )
    grad_pre, up_sums, grad_residual, grad_proj_pre, sums_two = mlp_call(
        mlp_backward_kernel,
        "mlp_backward",
        (grad_branch, down_full, slope, up_full, residual, proj_pre, given)
        + (gains[1:2], gains[2:3]),
        ("rows", "tall", "wide", "tall", "rows", "rows", "rows", "row", "row"),
        (bf16, f32, f32, bf16, f32),
        ("wide", "line", "rows", "rows", "sums"),
        *sizes,
        True,
    )
    grad_attended_t = dot(full_proj, grad_proj_pre, 1, 1).astype(bf16)
    given_high = to_heads(grad_attended_t[:, blk:])
    given_low = to_heads(grad_attended_t[:, :blk])

    grad_downward, grad_upward = mlp_call(
        mlp_grads_kernel,
        "mlp_grads",
        (hidden, grad_branch, grad_pre, normed_mid),
        ("wide", "rows", "wide", "rows"),
        (bf16, bf16),
        ("tall", "tall"),
        *sizes,
        False,
    )
    grad_proj = dot(attended_t, grad_proj_pre, 1, 0).astype(bf16)

    def own_rows(array):
        length = array.shape[0] // weight_parts
        return lax.dynamic_slice_in_dim(array, part * length, length, 0)

    early = jnp.concatenate(
        [
            up_sums[0],
            sums_three[2],
            sums_two[4],
            sums_two[0],
            sums_two[2],
            sums_three[0],
            sums_two[1],
            sums_two[3],
            sums_three[1],
        ]
    ).astype(bf16)
    grad_proj = jnp.concatenate([grad_proj, early.reshape(-1, model)], axis=0)
    given_high, grad_downward, grad_upward, grad_proj = lax.optimization_barrier(
        (given_high, grad_downward, grad_upward, grad_proj)
    )
    summed = lax.psum((grad_downward, grad_upward, grad_proj), everywhere)
    grad_downward, grad_upward, grad_proj = summed
    early = grad_proj[model:].astype(f32).reshape(-1)
    grad_proj = grad_proj[:model]
    grad_proj = own_rows(grad_proj).astype(f32)
    hidden_width = up_full.shape[0]
    grad_upbias = own_rows(early[:hidden_width])
    early = early[hidden_width:].reshape(8, model)
    grad_downbias = own_rows(early[0])
    grad_projbias = own_rows(early[1])

    def token_grads(array):
        own = lax.dynamic_slice_in_dim(array, group * HEADS, HEADS, 0)
        return lax.all_to_all(own, "h", 0, 0, tiled=True)

    grad_t, grad_n, delta, q_n = delta_rows(True, owner, given_high, out_high, q_t)
    high = (q_t[:, half:], q_n, grad_t, grad_n, log_high, delta)
    query_sum, high_pair = backward("high", owner, high, k_n, v_t, (), (), blk)
    high_tokens = token_grads(high_pair)
    grad_t, grad_n, delta, q_n = delta_rows(False, owner, given_low, out_low, q_t)
    low = (q_t[:, :half], q_n, grad_t, grad_n, log_low, delta)
    key_sum, value_sum, low_query = backward("low", owner, low, k_n, v_t, (), (), blk)
    starts = (query_sum, key_sum, value_sum, low_query)
    query_sum, first = backward("first", owner, high, k_n, v_t, starts, (high_tokens,), blk)
    first_tokens = token_grads(first)
    starts = (query_sum, key_sum, value_sum)
    query, second = backward("second", owner, high, k_n, v_t, starts, (), blk)
    query, first_tokens = lax.optimization_barrier((query, first_tokens))
    query_tokens = token_grads(query)

    def own_columns(array):
        length = array.shape[1] // weight_parts
        return lax.dynamic_slice_in_dim(array, part * length, length, 1)

    columns_grad, grad_downward, grad_upward = weight_grad(
        part.astype(jnp.int32),
        high_pair,
        first,
        query,
        second,
        a1_full,
        grad_downward,
        grad_upward,
        weight_parts,
        (first_tokens,),
    )
    columns_grad, query_tokens = lax.optimization_barrier((columns_grad, query_tokens))
    columns_grad = lax.all_to_all(columns_grad, "wt", 0, 0, tiled=True)
    columns_grad = jnp.sum(columns_grad.astype(f32), axis=0).astype(bf16)
    columns_grad, second = lax.optimization_barrier((columns_grad, second))
    second_tokens = token_grads(second)
    all_columns = lax.all_gather(columns_grad, "h", axis=0)
    grad_qkv = place(all_columns, width)
    sums = all_columns[:, 3 * width : 3 * width + 3, :width].astype(f32)
    sums = jnp.transpose(sums, (1, 0, 2)).reshape(3, model)
    grad_qvbias = own_rows(jnp.concatenate([sums[0], sums[2]]))

    own_weight = qkv_weight.astype(f32)
    shift_zero = jnp.sum(own_weight * sums.reshape(1, -1), axis=1)
    gain_zero = jnp.sum(own_weight * grad_qkv, axis=1)
    first_norm = own_columns(jnp.stack([gains[0], shifts[0]]))
    gain_zero = (gain_zero - first_norm[1] * shift_zero) / first_norm[0]

    input_grad = input_grads(
        first_tokens,
        second_tokens,
        query_tokens,
        high_tokens,
        full_qkv,
        activations.reshape(rows, model),
        grad_residual,
        gains[0:1],
    ).reshape(1, rows, model)
    early = own_columns(early)
    grad_gains = jnp.concatenate([gain_zero[None], early[2:5]], axis=0)
    grad_biases = jnp.concatenate([shift_zero[None], early[5:8]], axis=0)
    return (
        layer_output.reshape(1, rows, model),
        input_grad,
        grad_qkv,
        grad_qvbias,
        grad_proj,
        grad_projbias,
        grad_upward,
        grad_upbias,
        grad_downward,
        grad_downbias,
        grad_gains,
        grad_biases,
    )


def solution(mesh):
    groups = mesh.shape["ctx"] // HEADS
    split = Mesh(
        mesh.devices.reshape(groups, HEADS, mesh.shape["wt"]), ("r", "h", "wt")
    )
    tokens = P("wt", ("r", "h"), None)
    rows, flat, cols = P("wt", None), P("wt"), P(None, "wt")
    return jax.shard_map(
        functools.partial(local, groups),
        mesh=split,
        in_specs=(tokens, P(), rows, flat, rows, flat, rows, flat, rows, flat, cols, cols, tokens),
        out_specs=(tokens, tokens, rows, flat, rows, flat, rows, flat, rows, flat, cols, cols),
        check_vma=False,
    )
```

```python
import functools
import math

import jax
import jax.numpy as jnp
from jax import lax
from jax.experimental import pallas as pl
from jax.experimental.pallas import tpu as pltpu
from jax.sharding import Mesh
from jax.sharding import PartitionSpec as P

HEADS = 16
ALPHA = 32.0
EPS = 1e-05
NEG = -1e30
bf16 = jnp.bfloat16
f32 = jnp.float32
MIB = 1 << 20


def layer_norm(values, norm_gain, norm_shift):
    average = jnp.mean(values, axis=-1, keepdims=True)
    centered = values - average
    variance = jnp.mean(centered * centered, axis=-1, keepdims=True)
    return centered * lax.rsqrt(variance + EPS) * norm_gain + norm_shift


def gelu_and_slope(values):
    squared = values * values
    scale = math.sqrt(2.0 / math.pi)
    bent = jnp.tanh(scale * (values * (1.0 + 0.044715 * squared)))
    half = 0.5 * (1.0 + bent)
    slope = half + (0.5 * scale) * values * (1.0 - bent * bent) * (1.0 + 0.134145 * squared)
    return values * half, slope


def dot(a, b, ca, cb):
    return lax.dot_general(a, b, (((ca,), (cb,)), ((), ())), preferred_element_type=f32)


def columns(index, width):
    return pl.ds(pl.multiple_of(index * width, width), width)


def whole(shape):
    return pl.BlockSpec(shape, lambda *_: (0,) * len(shape), pipeline_mode=pl.Buffered(1))


def project_kernel(table, *refs):
    blocks, (weight, bias, q_t, k_n, v_t) = refs[:-5], refs[-5:]
    width = k_n.shape[1]
    for number, rows in enumerate(blocks):
        blk = rows.shape[0]
        part = slice(number * blk, (number + 1) * blk)
        heads = (dot(rows[...], weight[...], 1, 0) + bias[...]).astype(bf16)
        turned = jnp.transpose(heads[:, : 2 * width])
        q_t[:, part] = turned[:width]
        v_t[:, part] = turned[width:]
        k_n[part, :] = heads[:, 2 * width :]


def project(table, a1_full, weight, bias, blk, width):
    tokens, model = a1_full.shape
    count = 4
    tile = count * blk
    turned = pl.BlockSpec((width, tile), lambda i, t: (0, i))
    straight = pl.BlockSpec((tile, width), lambda i, t: (i, 0))

    def block(number):
        return pl.BlockSpec((blk, model), lambda i, t: (t[count * i + number], 0))

    return pl.pallas_call(
        project_kernel,
        grid_spec=pltpu.PrefetchScalarGridSpec(
            num_scalar_prefetch=1,
            grid=(tokens // tile,),
            in_specs=[block(number) for number in range(count)]
            + [whole(weight.shape), whole(bias.shape)],
            out_specs=[turned, straight, turned],
        ),
        out_shape=[
            jax.ShapeDtypeStruct((width, tokens), bf16),
            jax.ShapeDtypeStruct((tokens, width), bf16),
            jax.ShapeDtypeStruct((width, tokens), bf16),
        ],
        compiler_params=pltpu.CompilerParams(vmem_limit_bytes=48 * MIB),
        cost_estimate=pl.CostEstimate(
            flops=8 * tokens * model * width, bytes_accessed=2 * tokens * model, transcendentals=0
        ),
        name="project",
    )(table, *([a1_full] * count), weight, bias)


def forward_kernel(base, table, q_t, k_n, v_t, out_t, log_total, out_slots, scores):
    _, width, blk = out_slots.shape
    tile = q_t.shape[1]
    step = base + pl.program_id(0)
    query = q_t[...]

    def score(index):
        return dot(k_n[columns(index, blk), :], query, 1, 0)

    def prepare(index, slot):
        tile_scores = score(index)
        scores[slot] = tile_scores
        return jnp.max(tile_scores, axis=0, keepdims=True)

    ones = jnp.ones((16, blk), bf16)

    def absorb(index, tile_scores, peak, summed, tile_peak):
        new_peak = jnp.maximum(peak, tile_peak)
        weights = jnp.exp(tile_scores - new_peak).astype(bf16)
        keep = jnp.exp(peak - new_peak)
        values = jnp.concatenate([v_t[:, columns(index, blk)], ones], axis=0)
        return new_peak, summed * keep + dot(values, weights, 1, 0)

    def body(pair, carry):
        peak, summed, tile_peak = carry
        for slot in range(2):
            next_peak = prepare(2 * pair + slot + 1, 1 - slot)
            peak, summed = absorb(2 * pair + slot, scores[slot], peak, summed, tile_peak)
            tile_peak = next_peak
        return peak, summed, tile_peak

    carry = (
        jnp.full((1, tile), -jnp.inf, f32),
        jnp.zeros((width + 16, tile), f32),
        prepare(0, 0),
    )
    peak, summed, _ = lax.fori_loop(0, step, body, carry)
    for half in range(2):
        part = query[:, half * blk :]
        shape = (blk, tile - half * blk)
        key_pos = lax.broadcasted_iota(jnp.int32, shape, 0)
        query_pos = lax.broadcasted_iota(jnp.int32, shape, 1)
        tile_scores = dot(k_n[columns(2 * step + half, blk), :], part, 1, 0)
        tile_scores = jnp.where(query_pos >= key_pos, tile_scores, NEG)
        tile_peak = jnp.max(tile_scores, axis=0, keepdims=True)
        state = absorb(2 * step + half, tile_scores, peak, summed, tile_peak)
        if half == 0:
            left = tuple(array[:, :blk] for array in state)
            peak, summed = (array[:, blk:] for array in state)
    peak, summed = (
        jnp.concatenate([first, second], axis=1) for first, second in zip(left, state)
    )
    total = summed[width : width + 1]
    result = summed[:width] / total
    out_t[...] = result
    log_total[...] = peak + jnp.log(total)
    low = result.astype(bf16)
    for half in range(2):
        out_slots[table[2 * step + half]] = low[:, half * blk : (half + 1) * blk]


def forward(high, table, q_t, k_n, v_t, blk):
    width, tokens = q_t.shape
    slots = tokens // (2 * blk)
    tile = 2 * blk
    steps = slots // 2
    base = steps if high else 0
    seen = tokens if high else tokens // 2
    return pl.pallas_call(
        functools.partial(forward_kernel, base),
        grid_spec=pltpu.PrefetchScalarGridSpec(
            num_scalar_prefetch=1,
            grid=(steps,),
            in_specs=[
                pl.BlockSpec((width, tile), lambda i, t: (0, base + i)),
                whole((seen, width)),
                whole((width, seen)),
            ],
            out_specs=[
                pl.BlockSpec((width, tile), lambda i, t: (0, i)),
                pl.BlockSpec((1, tile), lambda i, t: (0, i)),
                whole((slots, width, blk)),
            ],
            scratch_shapes=[pltpu.VMEM((2, blk, tile), f32)],
        ),
        out_shape=[
            jax.ShapeDtypeStruct((width, tokens // 2), f32),
            jax.ShapeDtypeStruct((1, tokens // 2), f32),
            jax.ShapeDtypeStruct((slots, width, blk), bf16),
        ],
        compiler_params=pltpu.CompilerParams(vmem_limit_bytes=56 * MIB),
        cost_estimate=pl.CostEstimate(
            flops=(6 if high else 2) * tokens * tokens * width,
            bytes_accessed=12 * tokens * width,
            transcendentals=(3 if high else 1) * tokens * tokens // 8,
        ),
        name="forward_high" if high else "forward_low",
    )(table, q_t, k_n, v_t)


def delta_kernel(table, given, out_t, q_t, grad_t, grad_n, delta, q_n):
    block = given[0]
    grad_t[...] = block
    wide = block.astype(f32)
    delta[...] = jnp.sum(wide * out_t[...], axis=0, keepdims=True)
    grad_n[...] = jnp.transpose(wide).astype(bf16)
    q_n[...] = jnp.transpose(q_t[...].astype(f32)).astype(bf16)


def delta_rows(high, table, given, out_t, q_t):
    slots, width, blk = given.shape
    half = slots * blk
    base = slots if high else 0
    return pl.pallas_call(
        delta_kernel,
        grid_spec=pltpu.PrefetchScalarGridSpec(
            num_scalar_prefetch=1,
            grid=(slots,),
            in_specs=[
                pl.BlockSpec((1, width, blk), lambda p, t: (t[base + p], 0, 0)),
                pl.BlockSpec((width, blk), lambda p, t: (0, p)),
                pl.BlockSpec((width, blk), lambda p, t: (0, base + p)),
            ],
            out_specs=[
                pl.BlockSpec((width, blk), lambda p, t: (0, p)),
                pl.BlockSpec((blk, width), lambda p, t: (p, 0)),
                pl.BlockSpec((1, blk), lambda p, t: (0, p)),
                pl.BlockSpec((blk, width), lambda p, t: (p, 0)),
            ],
        ),
        out_shape=[
            jax.ShapeDtypeStruct((width, half), bf16),
            jax.ShapeDtypeStruct((half, width), bf16),
            jax.ShapeDtypeStruct((1, half), f32),
            jax.ShapeDtypeStruct((half, width), bf16),
        ],
        compiler_params=pltpu.CompilerParams(vmem_limit_bytes=32 * MIB),
        name="delta_high" if high else "delta_low",
    )(table, given, out_t, q_t)


def backward_kernel(kind, base, after, *refs):
    table, q_t, q_n, grad_t, grad_n, log_total, delta, k_n, v_t = refs[:9]
    refs = refs[9:]
    cross = kind in ("first", "second")
    query_out = key_out = value_out = None
    if cross:
        (query_start, key_start, value_start), refs = refs[:3], refs[3:]
    if kind == "first":
        low_query, refs = refs[0], refs[1:]
    refs = refs[after:]
    if kind == "second":
        query_slots, refs = refs[0], refs[1:]
    if kind in ("high", "first"):
        query_out, refs = refs[0], refs[1:]
    elif kind == "low":
        (key_out, value_out), refs = refs[:2], refs[2:]
    out_slots, refs = refs[0], refs[1:]
    scores, grads, query_sum, key_sum, value_sum = refs
    _, tile, blk = scores.shape
    slots = out_slots.shape[0]
    width = q_t.shape[0]
    piece = blk // 2
    step = pl.program_id(0)

    @pl.when(step == 0)
    def _():
        if cross:
            query_sum[...] = query_start[...]
        else:
            query_sum[...] = jnp.zeros_like(query_sum)
        if kind == "first":
            out_slots[:, :width] = low_query[...]

    keys = k_n[...].reshape(tile, width)
    keys_t = jnp.transpose(keys.astype(f32)).astype(bf16)
    if cross:
        start = piece if kind == "second" else 0
        starts = range(start, v_t.shape[1], blk)
        values = jnp.concatenate([v_t[:, at : at + piece] for at in starts], axis=1)
    else:
        values = v_t[...]
    values = jnp.transpose(values.astype(f32)).astype(bf16)
    if cross:
        key_sum[...] = key_start[...].reshape(tile, width)
        value_sum[...] = value_start[...].reshape(tile, width)
    else:
        key_sum[...] = jnp.zeros_like(key_sum)
        value_sum[...] = jnp.zeros_like(value_sum)

    def prepare(index, slot):
        at = columns(index, blk)
        scores[slot] = dot(keys, q_t[:, at], 1, 0)
        grads[slot] = dot(values, grad_t[:, at], 1, 0)

    def absorb(at, tile_scores, prob_grads):
        rows = tile_scores.shape[0]
        probs = jnp.exp(tile_scores - log_total[:, at])
        score_grads = (probs * (prob_grads - delta[:, at])).astype(bf16)
        value_sum[:rows] += dot(probs.astype(bf16), grad_n[at, :], 1, 0)
        key_sum[:rows] += dot(score_grads, q_n[at, :], 1, 0)
        query_sum[:, at] += dot(keys_t[:, :rows], score_grads, 1, 0)

    def diagonal(number):
        at = columns(4 * step + number, piece)
        shape = ((number + 1) * piece, piece)
        key_pos = lax.broadcasted_iota(jnp.int32, shape, 0)
        query_pos = number * piece + lax.broadcasted_iota(jnp.int32, shape, 1)
        tile_scores = dot(keys[: shape[0]], q_t[:, at], 1, 0)
        tile_scores = jnp.where(query_pos >= key_pos, tile_scores, NEG)
        absorb(at, tile_scores, dot(values[: shape[0]], grad_t[:, at], 1, 0))

    def sweep(first, pairs):
        prepare(first, 0)

        def body(pair, carry):
            index = first + 2 * pair
            prepare(index + 1, 1)
            absorb(columns(index, blk), scores[0], grads[0])
            prepare(jnp.minimum(index + 2, slots - 1), 0)
            absorb(columns(index + 1, blk), scores[1], grads[1])
            return carry

        lax.fori_loop(0, pairs, body, 0)

    if cross:
        sweep(0, slots // 2)
    else:
        for number in range(4):
            diagonal(number)

        @pl.when(2 * step + 2 < slots)
        def _():
            sweep(2 * step + 2, slots // 2 - 1 - step)

    def query_grads(index):
        return (query_sum[:, columns(index, blk)] * 0.125).astype(bf16)

    if kind == "low":
        key_out[...] = key_sum[...]
        value_out[...] = value_sum[...]
        for half in range(2):
            index = 2 * step + half
            out_slots[table[base + index]] = query_grads(index)
    else:
        key_t = jnp.transpose(key_sum[...]).astype(bf16)
        value_t = jnp.transpose(value_sum[...]).astype(bf16)
        wide = blk if kind == "high" else piece
        for number in range(tile // wide):
            slot = table[base + tile // wide * step + number]
            part = slice(number * wide, (number + 1) * wide)
            if kind == "first":
                out_slots[slot, width:, :piece] = key_t[:, part]
                out_slots[slot, width:, piece:] = value_t[:, part]
            else:
                out_slots[slot, :width] = key_t[:, part]
                out_slots[slot, width:] = value_t[:, part]

    @pl.when(step == pl.num_programs(0) - 1)
    def _():
        if query_out is not None:
            query_out[...] = query_sum[...]
        if kind == "second":

            def finish(index, carry):
                query_slots[table[slots + index]] = query_grads(index)
                return carry

            lax.fori_loop(0, slots, finish, 0)


def backward(kind, table, queries, k_n, v_t, starts, after, blk):
    width, half = queries[0].shape
    slots = half // blk
    tile = 2 * blk
    piece = blk // 2
    cross = kind in ("first", "second")
    second = 1 if kind == "second" else 0
    steps = slots // 4 if cross else slots // 2
    skip = slots // 2 if kind == "high" else 0
    if cross:
        straight = pl.BlockSpec((4, 1, piece, width), lambda i, t: (i, second, 0, 0))
        k_n = k_n.reshape(-1, 2, piece, width)
        starts = (
            (starts[0],)
            + tuple(array.reshape(-1, 2, piece, width) for array in starts[1:3])
            + tuple(starts[3:])
        )
    else:
        straight = pl.BlockSpec((tile, width), lambda i, t: (skip + i, 0))
    in_specs = [whole(array.shape) for array in queries] + [
        straight,
        pl.BlockSpec((width, 4 * blk if cross else tile), lambda i, t: (0, skip + i)),
    ]
    if cross:
        in_specs += [whole((width, half)), straight, straight]
        in_specs += [whole(array.shape) for array in starts[3:]]
    in_specs += [pl.BlockSpec(memory_space=pl.ANY)] * len(after)
    rows = width if kind == "low" else 2 * width
    held = (slots, rows, piece if kind == "second" else blk)
    out_specs = [whole(held)]
    out_shape = [jax.ShapeDtypeStruct(held, bf16)]
    if kind in ("high", "first"):
        out_specs = [whole((width, half))] + out_specs
        out_shape = [jax.ShapeDtypeStruct((width, half), f32)] + out_shape
    elif kind == "second":
        out_specs = [whole((slots, width, blk))] + out_specs
        out_shape = [jax.ShapeDtypeStruct((slots, width, blk), bf16)] + out_shape
    elif kind == "low":
        out_specs = [straight, straight] + out_specs
        out_shape = [jax.ShapeDtypeStruct((half, width), f32)] * 2 + out_shape
    return pl.pallas_call(
        functools.partial(backward_kernel, kind, 2 * skip, len(after)),
        grid_spec=pltpu.PrefetchScalarGridSpec(
            num_scalar_prefetch=1,
            grid=(steps,),
            in_specs=in_specs,
            out_specs=out_specs,
            scratch_shapes=[
                pltpu.VMEM((2, tile, blk), f32),
                pltpu.VMEM((2, tile, blk), f32),
                pltpu.VMEM((width, half), f32),
                pltpu.VMEM((tile, width), f32),
                pltpu.VMEM((tile, width), f32),
            ],
        ),
        out_shape=out_shape,
        compiler_params=pltpu.CompilerParams(vmem_limit_bytes=56 * MIB),
        cost_estimate=pl.CostEstimate(
            flops=4 * half * half * width,
            bytes_accessed=32 * half * width,
            transcendentals=half * half // 8,
        ),
        name="backward_" + kind,
    )(table, *queries, k_n, v_t, *starts, *after)


def weight_kernel(high_pair, first, query, second, a1, *refs):
    out, total, sums = refs[-3:]
    _, width, blk = query.shape
    piece = blk // 2
    parts, rows, length = out.shape
    step = pl.program_id(0)

    @pl.when(step == 0)
    def _():
        total[...] = jnp.zeros_like(total)
        sums[...] = jnp.zeros_like(sums)

    low_key = jnp.concatenate([first[0, width:, :piece], second[0, :width]], axis=1)
    low_value = jnp.concatenate([first[0, width:, piece:], second[0, width:]], axis=1)
    low = jnp.concatenate([first[0, :width], low_key, low_value], axis=0)
    high = jnp.concatenate([query[0], high_pair[0]], axis=0)
    total[...] += dot(low, a1[:blk], 1, 0) + dot(high, a1[blk:], 1, 0)
    wide = low.astype(f32) + high.astype(f32)
    for at in range(0, blk, 128):
        sums[...] += wide[:, at : at + 128]

    @pl.when(step == pl.num_programs(0) - 1)
    def _():
        row = jnp.sum(jnp.transpose(sums[...]), axis=0, keepdims=True)
        tail = [row[:, number * width : (number + 1) * width] for number in range(3)]
        tail = jnp.concatenate(tail, axis=0)
        tail = jnp.concatenate([tail, jnp.zeros((3, length - width), f32)], axis=1)
        tail = jnp.concatenate([tail, jnp.zeros((rows - 3 * width - 3, length), f32)], axis=0)
        for number in range(parts):
            own = total[:, number * length : (number + 1) * length]
            out[number] = jnp.concatenate([own, tail], axis=0).astype(bf16)


def weight_grad(high_pair, first, query, second, a1_full, parts, after):
    slots, width, blk = query.shape
    tokens, model = a1_full.shape
    rows = 3 * width
    shape = (parts, rows + 16, model // parts)
    given = (high_pair, first, query, second)
    return pl.pallas_call(
        weight_kernel,
        grid=(slots,),
        in_specs=[pl.BlockSpec((1,) + array.shape[1:], lambda s: (s, 0, 0)) for array in given]
        + [pl.BlockSpec((2 * blk, model), lambda s: (s, 0))]
        + [pl.BlockSpec(memory_space=pl.ANY)] * len(after),
        out_specs=whole(shape),
        out_shape=jax.ShapeDtypeStruct(shape, bf16),
        scratch_shapes=[pltpu.VMEM((rows, model), f32), pltpu.VMEM((rows, 128), f32)],
        compiler_params=pltpu.CompilerParams(vmem_limit_bytes=48 * MIB),
        cost_estimate=pl.CostEstimate(
            flops=2 * rows * tokens * model, bytes_accessed=2 * tokens * model, transcendentals=0
        ),
        name="weight_grad",
    )(*given, a1_full, *after)


def normalize(values):
    centered = values - jnp.mean(values, axis=-1, keepdims=True)
    factor = lax.rsqrt(jnp.mean(centered * centered, axis=-1, keepdims=True) + EPS)
    return centered * factor, factor


def normalize_backward(normal, factor, gain, upstream):
    scaled = upstream * gain
    along = jnp.mean(scaled * normal, axis=-1, keepdims=True)
    return factor * (scaled - jnp.mean(scaled, axis=-1, keepdims=True) - normal * along)


def over_rows(rows, body, count, width):
    strip = 128

    def one(index, sums):
        return body(pl.ds(pl.multiple_of(index * strip, strip), strip), sums)

    zero = tuple(jnp.zeros((1, width), f32) for _ in range(count))
    return lax.fori_loop(0, rows // strip, one, zero)


def column_sum(values):
    return jnp.sum(values, axis=0, keepdims=True)


def mlp_forward_kernel(
    normed, up, up_bias, down, down_bias, residual, upstream, gain, shift,
    hidden, slope, layer_output, grad_branch, sums, total,
):
    step = pl.program_id(0)

    @pl.when(step == 0)
    def _():
        total[...] = jnp.zeros_like(total)

    value, bend = gelu_and_slope(dot(normed[...], up[...], 1, 1) + up_bias[...])
    low = value.astype(bf16)
    hidden[...] = low
    slope[...] = bend.astype(bf16)
    total[...] += dot(low, down[...], 1, 0)

    @pl.when(step == pl.num_programs(0) - 1)
    def _():
        def strip(at, carry):
            normal, factor = normalize(total[at, :] + down_bias[...])
            output = residual[at, :] + normal * gain[...] + shift[...]
            layer_output[at, :] = output.astype(bf16)
            given = upstream[at, :].astype(f32)
            grad = normalize_backward(normal, factor, gain[...], given).astype(bf16)
            grad_branch[at, :] = grad
            new = (given * normal, given, grad.astype(f32))
            return tuple(old + column_sum(part) for old, part in zip(carry, new))

        result = over_rows(*[total.shape[0], strip, 3, total.shape[1]])
        for number in range(3):
            sums[number : number + 1] = result[number]


def mlp_backward_kernel(
    grad, down, slope, up, residual, proj_pre, upstream, gain_one, gain_two,
    grad_pre, up_sums, grad_residual, grad_proj_pre, sums, total,
):
    step = pl.program_id(0)

    @pl.when(step == 0)
    def _():
        total[...] = jnp.zeros_like(total)

    low = (dot(grad[...], down[...], 1, 1) * slope[...].astype(f32)).astype(bf16)
    grad_pre[...] = low
    up_sums[...] = column_sum(low.astype(f32))
    total[...] += dot(low, up[...], 1, 0)

    @pl.when(step == pl.num_programs(0) - 1)
    def _():
        def strip(at, carry):
            grad_mid = total[at, :]
            normal_two, factor = normalize(residual[at, :])
            back = normalize_backward(normal_two, factor, gain_two[...], grad_mid)
            back = upstream[at, :].astype(f32) + back
            grad_residual[at, :] = back
            normal_one, factor = normalize(proj_pre[at, :])
            low = normalize_backward(normal_one, factor, gain_one[...], back).astype(bf16)
            grad_proj_pre[at, :] = low
            new = (back * normal_one, back, grad_mid * normal_two, grad_mid, low.astype(f32))
            return tuple(old + column_sum(part) for old, part in zip(carry, new))

        result = over_rows(*[total.shape[0], strip, 5, total.shape[1]])
        for number in range(5):
            sums[number : number + 1] = result[number]


def mlp_grads_kernel(hidden, grad, grad_pre, normed, down_out, up_out):
    down_out[...] = dot(hidden[...], grad[...], 0, 0).astype(bf16)
    up_out[...] = dot(grad_pre[...], normed[...], 0, 0).astype(bf16)


def mlp_call(kernel, name, operands, kinds, results, result_kinds, rows, model, hidden, kept):
    chunk = 512
    specs = {
        "rows": whole((rows, model)),
        "wide": pl.BlockSpec((rows, chunk), lambda j: (0, j)),
        "tall": pl.BlockSpec((chunk, model), lambda j: (j, 0)),
        "line": pl.BlockSpec((1, chunk), lambda j: (0, j)),
        "row": whole((1, model)),
        "sums": whole((8, model)),
    }
    shapes = {
        "rows": (rows, model),
        "wide": (rows, hidden),
        "tall": (hidden, model),
        "line": (1, hidden),
        "sums": (8, model),
    }
    return pl.pallas_call(
        kernel,
        grid=(hidden // chunk,),
        in_specs=[specs[kind] for kind in kinds],
        out_specs=[specs[kind] for kind in result_kinds],
        out_shape=[
            jax.ShapeDtypeStruct(shapes[kind], dtype) for kind, dtype in zip(result_kinds, results)
        ],
        scratch_shapes=[pltpu.VMEM((rows, model), f32)] if kept else [],
        compiler_params=pltpu.CompilerParams(vmem_limit_bytes=56 * MIB),
        cost_estimate=pl.CostEstimate(
            flops=4 * rows * model * hidden, bytes_accessed=8 * rows * hidden, transcendentals=0
        ),
        name=name,
    )(*operands)


def input_kernel(
    first, second, query, high, weight_q, weight_k, weight_v, inputs, grad_residual, gain,
    out, total,
):
    step = pl.program_id(0)
    heads, _, blk = first.shape
    width = query.shape[1]
    piece = blk // 2
    rows = heads * width

    def part(array, start):
        return array[:, start : start + width].reshape(rows, array.shape[2])

    @pl.when(step == 0)
    def _():
        total[...] = jnp.zeros_like(total)

    weight = jnp.concatenate([weight_q[...], weight_k[...], weight_v[...]], axis=1)
    pair = part(first, width)
    key = jnp.concatenate([pair[:, :piece], part(second, 0)], axis=1)
    value = jnp.concatenate([pair[:, piece:], part(second, width)], axis=1)
    low = jnp.concatenate([part(first, 0), key, value], axis=0)
    top = jnp.concatenate([part(query, 0), part(high, 0), part(high, width)], axis=0)
    total[:, :blk] += dot(weight, low, 1, 0)
    total[:, blk:] += dot(weight, top, 1, 0)

    @pl.when(step == pl.num_programs(0) - 1)
    def _():
        def strip(index, carry):
            at = columns(index, 128)
            grad = jnp.transpose(total[:, at])
            normal, factor = normalize(inputs[at, :].astype(f32))
            back = normalize_backward(normal, factor, gain[...], grad)
            out[at, :] = grad_residual[at, :] + back
            return carry

        lax.fori_loop(0, out.shape[0] // 128, strip, 0)


def input_grads(first, second, query, high, weight, inputs, grad_residual, gain):
    heads, width, blk = query.shape
    rows, model = inputs.shape
    count = 4
    steps = heads // count
    given = (first, second, query, high)

    def columns_of(number):
        return pl.BlockSpec((model, count * width), lambda j: (0, number * steps + j))

    return pl.pallas_call(
        input_kernel,
        grid=(steps,),
        in_specs=[pl.BlockSpec((count,) + array.shape[1:], lambda j: (j, 0, 0)) for array in given]
        + [columns_of(number) for number in range(3)]
        + [whole((rows, model)), whole((rows, model)), whole((1, model))],
        out_specs=whole((rows, model)),
        out_shape=jax.ShapeDtypeStruct((rows, model), f32),
        scratch_shapes=[pltpu.VMEM((model, rows), f32)],
        compiler_params=pltpu.CompilerParams(vmem_limit_bytes=56 * MIB),
        cost_estimate=pl.CostEstimate(
            flops=6 * rows * model * model, bytes_accessed=24 * rows * model, transcendentals=0
        ),
        name="input_grads",
    )(*given, weight, weight, weight, inputs, grad_residual, gain)


def place_kernel(given, out):
    count, width, length = given.shape
    out[...] = jnp.transpose(given[...].reshape(count * width, length)).astype(f32)


def place(gathered, width):
    heads, _, length = gathered.shape
    count = 4
    groups = heads // count
    return pl.pallas_call(
        place_kernel,
        grid=(3, groups),
        in_specs=[pl.BlockSpec((count, width, length), lambda c, i: (i, c, 0))],
        out_specs=pl.BlockSpec((length, count * width), lambda c, i: (0, c * groups + i)),
        out_shape=jax.ShapeDtypeStruct((length, 3 * heads * width), f32),
        compiler_params=pltpu.CompilerParams(vmem_limit_bytes=32 * MIB),
        name="place",
    )(gathered)


def local(
    groups,
    activations,
    block_order,
    qkv_weight,
    qv_bias,
    proj_weight,
    proj_bias,
    up_weight,
    up_bias,
    down_weight,
    down_bias,
    norm_gains,
    norm_biases,
    cotangent,
):
    _, rows, model = activations.shape
    blk = rows // 2
    width = model // HEADS
    ctx = ("r", "h")
    everywhere = ("r", "h", "wt")
    devices = groups * HEADS
    weight_parts = lax.axis_size("wt")
    head = lax.axis_index("h")
    group = lax.axis_index("r")
    part = lax.axis_index("wt")

    small = (qv_bias, proj_bias, up_bias, down_bias, norm_gains, norm_biases)
    packed = jnp.concatenate([array.reshape(-1) for array in small])
    gathered = lax.all_gather(packed, "wt", axis=0)
    pieces, start = [], 0
    for array in small:
        piece = gathered[:, start : start + array.size].reshape((weight_parts,) + array.shape)
        start += array.size
        if array.ndim == 2:
            piece = jnp.transpose(piece, (1, 0, 2)).reshape(array.shape[0], -1)
        else:
            piece = piece.reshape(-1)
        pieces.append(piece.astype(f32))
    qvbias, projbias, upbias, downbias, gains, shifts = pieces

    inputs = activations.reshape(rows, model).astype(f32)
    a1 = layer_norm(inputs, gains[0], shifts[0]).astype(bf16)
    a1_full = lax.all_gather(a1, ctx, axis=0, tiled=True)

    mine = lax.dynamic_index_in_dim(
        qkv_weight.reshape(-1, 3, HEADS, width), head, axis=2, keepdims=False
    )
    mine = lax.all_gather(mine.reshape(-1, 3 * width), "wt", axis=0, tiled=True)
    scale = 1.0 / math.sqrt(width)
    mine = jnp.concatenate(
        [mine[:, :width] * bf16(scale), mine[:, 2 * width :], mine[:, width : 2 * width]], axis=1
    )
    q_bias = lax.dynamic_slice(qvbias, (head * width,), (width,))
    v_bias = lax.dynamic_slice(qvbias, (model + head * width,), (width,))
    bias = jnp.concatenate([q_bias * scale, v_bias, jnp.zeros_like(q_bias)])

    lows = block_order.reshape(devices, 2)[:, 0]
    numbers = jnp.arange(devices, dtype=jnp.int32)
    owner = jnp.sum(jnp.where(lows[None, :] == numbers[:, None], numbers[None, :], 0), axis=1)
    owner = jnp.concatenate([owner, owner[::-1]]).astype(jnp.int32)
    is_high = (jnp.arange(2 * devices, dtype=jnp.int32) >= devices).astype(jnp.int32)
    slot_of = 2 * owner + is_high

    half = devices * blk
    q_t, k_n, v_t = project(slot_of, a1_full, mine, bias[None, :], blk, width)
    out_low, log_low, slots_low = forward(False, owner, q_t, k_n, v_t, blk)
    out_high, log_high, slots_high = forward(True, owner, q_t, k_n, v_t, blk)

    def to_tokens(array):
        own = lax.dynamic_slice_in_dim(array, group * HEADS, HEADS, 0)
        return lax.all_to_all(own, "h", 0, 0, tiled=True).reshape(-1, blk)

    def to_heads(array):
        array = lax.all_to_all(array.reshape(HEADS, width, blk), "h", 0, 0, tiled=True)
        if groups > 1:
            array = lax.all_gather(array, "r", axis=0, tiled=True)
        return array

    attended_t = jnp.concatenate([to_tokens(slots_low), to_tokens(slots_high)], axis=1)

    full_proj = lax.all_gather(proj_weight, "wt", axis=0, tiled=True)
    up_full = lax.all_gather(up_weight, "wt", axis=0, tiled=True)
    down_full = lax.all_gather(down_weight, "wt", axis=0, tiled=True)
    full_qkv = lax.all_gather(qkv_weight, "wt", axis=0, tiled=True)

    proj_pre = dot(attended_t, full_proj, 0, 0) + projbias
    residual = inputs + layer_norm(proj_pre, gains[1], shifts[1])
    normed_mid = layer_norm(residual, gains[2], shifts[2]).astype(bf16)
    sizes = (rows, model, up_full.shape[0])
    given = cotangent.reshape(rows, model)
    hidden, slope, layer_output, grad_branch, sums_three = mlp_call(
        mlp_forward_kernel,
        "mlp_forward",
        (normed_mid, up_full, upbias[None, :], down_full, downbias[None, :], residual, given)
        + (gains[3:4], shifts[3:4]),
        ("rows", "tall", "line", "tall", "row", "rows", "rows", "row", "row"),
        (bf16, bf16, bf16, bf16, f32),
        ("wide", "wide", "rows", "rows", "sums"),
        *sizes,
        True,
    )
    grad_pre, up_sums, grad_residual, grad_proj_pre, sums_two = mlp_call(
        mlp_backward_kernel,
        "mlp_backward",
        (grad_branch, down_full, slope, up_full, residual, proj_pre, given)
        + (gains[1:2], gains[2:3]),
        ("rows", "tall", "wide", "tall", "rows", "rows", "rows", "row", "row"),
        (bf16, f32, f32, bf16, f32),
        ("wide", "line", "rows", "rows", "sums"),
        *sizes,
        True,
    )
    grad_attended_t = dot(full_proj, grad_proj_pre, 1, 1).astype(bf16)
    given_high = to_heads(grad_attended_t[:, blk:])
    given_low = to_heads(grad_attended_t[:, :blk])

    grad_downward, grad_upward = mlp_call(
        mlp_grads_kernel,
        "mlp_grads",
        (hidden, grad_branch, grad_pre, normed_mid),
        ("wide", "rows", "wide", "rows"),
        (bf16, bf16),
        ("tall", "tall"),
        *sizes,
        False,
    )
    grad_proj = dot(attended_t, grad_proj_pre, 1, 0).astype(bf16)

    def own_rows(array):
        length = array.shape[0] // weight_parts
        return lax.dynamic_slice_in_dim(array, part * length, length, 0)

    early = jnp.concatenate(
        [
            up_sums[0],
            sums_three[2],
            sums_two[4],
            sums_two[0],
            sums_two[2],
            sums_three[0],
            sums_two[1],
            sums_two[3],
            sums_three[1],
        ]
    ).astype(bf16)
    grad_proj = jnp.concatenate([grad_proj, early.reshape(-1, model)], axis=0)
    given_high, grad_downward, grad_upward, grad_proj = lax.optimization_barrier(
        (given_high, grad_downward, grad_upward, grad_proj)
    )
    summed = lax.psum((grad_downward, grad_upward, grad_proj), everywhere)
    grad_downward, grad_upward, grad_proj = summed
    early = grad_proj[model:].astype(f32).reshape(-1)
    grad_proj = grad_proj[:model]
    grad_proj = own_rows(grad_proj).astype(f32)
    hidden_width = up_full.shape[0]
    grad_upbias = own_rows(early[:hidden_width])
    early = early[hidden_width:].reshape(8, model)
    grad_downbias = own_rows(early[0])
    grad_projbias = own_rows(early[1])

    def token_grads(array):
        own = lax.dynamic_slice_in_dim(array, group * HEADS, HEADS, 0)
        return lax.all_to_all(own, "h", 0, 0, tiled=True)

    grad_t, grad_n, delta, q_n = delta_rows(True, owner, given_high, out_high, q_t)
    high = (q_t[:, half:], q_n, grad_t, grad_n, log_high, delta)
    query_sum, high_pair = backward("high", owner, high, k_n, v_t, (), (), blk)
    high_tokens = token_grads(high_pair)
    grad_t, grad_n, delta, q_n = delta_rows(False, owner, given_low, out_low, q_t)
    low = (q_t[:, :half], q_n, grad_t, grad_n, log_low, delta)
    key_sum, value_sum, low_query = backward("low", owner, low, k_n, v_t, (), (), blk)
    starts = (query_sum, key_sum, value_sum, low_query)
    query_sum, first = backward("first", owner, high, k_n, v_t, starts, (high_tokens,), blk)
    first_tokens = token_grads(first)
    starts = (query_sum, key_sum, value_sum)
    query, second = backward("second", owner, high, k_n, v_t, starts, (), blk)
    query, first_tokens = lax.optimization_barrier((query, first_tokens))
    query_tokens = token_grads(query)

    def own_columns(array):
        length = array.shape[1] // weight_parts
        return lax.dynamic_slice_in_dim(array, part * length, length, 1)

    columns_grad = weight_grad(
        high_pair, first, query, second, a1_full, weight_parts, (first_tokens,) + tuple(summed)
    )
    grad_downward = own_rows(grad_downward).astype(f32)
    grad_upward = own_rows(grad_upward).astype(f32)
    columns_grad, query_tokens = lax.optimization_barrier((columns_grad, query_tokens))
    columns_grad = lax.all_to_all(columns_grad, "wt", 0, 0, tiled=True)
    columns_grad = jnp.sum(columns_grad.astype(f32), axis=0).astype(bf16)
    columns_grad, second = lax.optimization_barrier((columns_grad, second))
    second_tokens = token_grads(second)
    all_columns = lax.all_gather(columns_grad, "h", axis=0)
    grad_qkv = place(all_columns, width)
    sums = all_columns[:, 3 * width : 3 * width + 3, :width].astype(f32)
    sums = jnp.transpose(sums, (1, 0, 2)).reshape(3, model)
    grad_qvbias = own_rows(jnp.concatenate([sums[0], sums[2]]))

    own_weight = qkv_weight.astype(f32)
    shift_zero = jnp.sum(own_weight * sums.reshape(1, -1), axis=1)
    gain_zero = jnp.sum(own_weight * grad_qkv, axis=1)
    first_norm = own_columns(jnp.stack([gains[0], shifts[0]]))
    gain_zero = (gain_zero - first_norm[1] * shift_zero) / first_norm[0]

    input_grad = input_grads(
        first_tokens,
        second_tokens,
        query_tokens,
        high_tokens,
        full_qkv,
        activations.reshape(rows, model),
        grad_residual,
        gains[0:1],
    ).reshape(1, rows, model)
    early = own_columns(early)
    grad_gains = jnp.concatenate([gain_zero[None], early[2:5]], axis=0)
    grad_biases = jnp.concatenate([shift_zero[None], early[5:8]], axis=0)
    return (
        layer_output.reshape(1, rows, model),
        input_grad,
        grad_qkv,
        grad_qvbias,
        grad_proj,
        grad_projbias,
        grad_upward,
        grad_upbias,
        grad_downward,
        grad_downbias,
        grad_gains,
        grad_biases,
    )


def solution(mesh):
    groups = mesh.shape["ctx"] // HEADS
    split = Mesh(
        mesh.devices.reshape(groups, HEADS, mesh.shape["wt"]), ("r", "h", "wt")
    )
    tokens = P("wt", ("r", "h"), None)
    rows, flat, cols = P("wt", None), P("wt"), P(None, "wt")
    return jax.shard_map(
        functools.partial(local, groups),
        mesh=split,
        in_specs=(tokens, P(), rows, flat, rows, flat, rows, flat, rows, flat, cols, cols, tokens),
        out_specs=(tokens, tokens, rows, flat, rows, flat, rows, flat, rows, flat, cols, cols),
        check_vma=False,
    )
```
